128 devices in a mesh: doc: 4 (over y), resp: 8 (over z, x_hi), prob: 4 (over x_lo, core).
Axes of the slice: x: 4 (x_hi: 2, x_lo: 2; x = x_hi * 2 + x_lo), y: 4, z: 4, core: 2. Of those that a mesh axis runs over, the one named last changes fastest.
Arguments:
- x_doc: bfloat16 [512, 5120], P('doc'), may hold values from -6 to 6
- x_prompt: bfloat16 [4, 1024, 5120], P('prob', 'resp'), may hold values from -6 to 6
- w_key: bfloat16 [5120, 512], replicated, may hold values from -0.078125 to 0.078125
- w_value: bfloat16 [5120, 512], replicated, may hold values from -0.078125 to 0.078125
- queries: bfloat16 [128, 128, 4096], P(('doc', 'resp', 'prob')), may hold values from -240 to 240
- resp_keys: bfloat16 [128, 128, 512], P(('doc', 'resp', 'prob')), may hold values from -6 to 6
- resp_values: bfloat16 [128, 128, 512], P(('doc', 'resp', 'prob')), may hold values from -6 to 6
- out_grad: bfloat16 [128, 128, 4096], P(('doc', 'resp', 'prob')), may hold values from -6 to 6
- lengths: int32 [128], P(('doc', 'resp', 'prob')), may hold values from 64 to 128, as said below
Outputs:
- grad_queries: bfloat16 [128, 128, 4096], P(('doc', 'resp', 'prob'))
- grad_keys: bfloat16 [128, 128, 512], P(('doc', 'resp', 'prob'))
- grad_values: bfloat16 [128, 128, 512], P(('doc', 'resp', 'prob'))
- grad_doc: bfloat16 [512, 5120], P('doc')
- grad_prompt: bfloat16 [4, 1024, 5120], P('prob', 'resp')
The draws below stay inside these ranges and needn't reach their ends.
Inputs may be any that keep to these rules, and one draw needn't show every extreme that they name: `lengths`: token slots at or beyond a response's length are padding.
All inputs are finite; a program needn't handle non-finite values.
Results may differ from the reference program's by a relative error of at most 0.0085.
Values may be sent and summed in bfloat16 or wider, within the bound.
No kernel may reach another device: no remote copies, remote signals or barrier semaphores. Data moves between devices by JAX's collectives and lax.ppermute only.
A program may use at most 128 MiB of HBM per device.

```python
import jax
import jax.numpy as jnp
from jax import lax

D = 5120
QH = 32
KVH = 4
HD = 128
R = 128
GROUP = 8
DOC = 512
PROMPT = 1024
PROBLEMS = 4
RESPONSES = 128
KEYS = 1664


def common_keys(key):
    return jnp.clip(jax.random.normal(key, (RESPONSES, R, KVH * HD), jnp.float32), -6.0, 6.0)


def draw_resp_keys(key, part):
    base = common_keys(key)
    return base.astype(jnp.bfloat16)


def draw_queries(key, part):
    key = jax.random.fold_in(key, 5)
    fresh = jnp.clip(jax.random.normal(key, (RESPONSES, R, QH * HD), jnp.float32), -6.0, 6.0)
    return fresh.astype(jnp.bfloat16)


def draw_lengths(key, part):
    key = jax.random.fold_in(key, 9)
    drawn = jax.random.randint(key, (RESPONSES,), R // 2, R + 1, dtype=jnp.int32)
    return drawn.at[0].set(R)


def steps_of(stream_key, shape, split, least, top_value):
    def one(axis_at, shards_of):
        steps = jax.random.uniform(jax.random.fold_in(jax.random.fold_in(stream_key, 6), axis_at), (shards_of,), jnp.float32, least / len(split), top_value / len(split))
        return jnp.repeat(jnp.exp(steps), shape[axis_at] // shards_of).reshape((-1,) + (1,) * (len(shape) - axis_at - 1))

    gain = one(*split[0])
    for cut in split[1:]:
        gain = gain * one(*cut)
    return gain


def bell_draw(own_key, dims, deviation, bound, cuts=(), kind=jnp.bfloat16):
    values = deviation * jax.random.normal(own_key, dims, jnp.float32)
    if cuts:
        values = values * steps_of(own_key, dims, cuts, -0.22, 0.18)
    return jnp.clip(values, -bound, bound).astype(kind)


def setup_inputs(seed: int = 0) -> dict:
    splits = jax.random.split(jax.random.key(seed), 10)
    return {
        "x_doc": bell_draw(splits[0], (DOC, D), 1.0, 6.0, ((0, 4),)),
        "x_prompt": bell_draw(splits[1], (PROBLEMS, PROMPT, D), 1.0, 6.0, ((0, 4), (1, 8))),
        "w_key": bell_draw(splits[2], (D, KVH * HD), D ** -0.5, 0.078125),
        "w_value": bell_draw(splits[3], (D, KVH * HD), D ** -0.5, 0.078125),
        "queries": draw_queries(jax.random.fold_in(splits[9], 71), 0),
        "resp_keys": draw_resp_keys(jax.random.fold_in(splits[9], 71), 0),
        "resp_values": bell_draw(splits[6], (RESPONSES, R, KVH * HD), 1.0, 6.0, ((0, 128),)),
        "out_grad": bell_draw(splits[7], (RESPONSES, R, QH * HD), 1.0, 6.0, ((0, 128),)),
        "lengths": draw_lengths(jax.random.fold_in(splits[9], 71), 0),
    }


def attend(q, cot, keys, values, length):
    scale = 1.0 / (HD ** 0.5)
    pre = DOC + PROMPT
    rows = jnp.arange(R, dtype=jnp.int32)
    cols = jnp.arange(KEYS, dtype=jnp.int32)
    later = cols - pre
    allowed = (cols[None, :] < pre) | ((later[None, :] <= rows[:, None]) & (later[None, :] < length))
    qh = q.reshape(R, KVH, GROUP, HD).astype(jnp.float32)
    gh = cot.reshape(R, KVH, GROUP, HD).astype(jnp.float32)
    kh = keys.reshape(KEYS, KVH, HD).astype(jnp.float32)
    vh = values.reshape(KEYS, KVH, HD).astype(jnp.float32)
    scores = jnp.einsum('tngd,knd->ngtk', qh, kh) * scale
    scores = jnp.where(allowed, scores, -1e30)
    peak = jnp.max(scores, axis=-1, keepdims=True)
    expo = jnp.exp(scores - peak)
    probs = expo / jnp.sum(expo, axis=-1, keepdims=True)
    probs_b = lax.optimization_barrier(probs.astype(jnp.bfloat16)).astype(jnp.float32)
    dprob = jnp.einsum('tngd,knd->ngtk', gh, vh)
    delta = jnp.sum(probs * dprob, axis=-1, keepdims=True)
    dscore = lax.optimization_barrier((probs * (dprob - delta) * scale).astype(jnp.bfloat16)).astype(jnp.float32)
    dq = jnp.einsum('ngtk,knd->tngd', dscore, kh).reshape(R, QH * HD).astype(jnp.bfloat16)
    dk = jnp.einsum('ngtk,tngd->knd', dscore, qh).reshape(KEYS, KVH * HD)
    dv = jnp.einsum('ngtk,tngd->knd', probs_b, gh).reshape(KEYS, KVH * HD)
    return dq, dk, dv


def reference(x_doc, x_prompt, w_key, w_value, queries, resp_keys, resp_values, out_grad, lengths):
    width = KVH * HD
    pre = DOC + PROMPT
    doc_k = jnp.dot(x_doc, w_key, preferred_element_type=jnp.float32).astype(jnp.bfloat16)
    doc_v = jnp.dot(x_doc, w_value, preferred_element_type=jnp.float32).astype(jnp.bfloat16)
    flat_prompt = x_prompt.reshape(PROBLEMS * PROMPT, D)
    prompt_k = jnp.dot(flat_prompt, w_key, preferred_element_type=jnp.float32).astype(jnp.bfloat16).reshape(PROBLEMS, PROMPT, width)
    prompt_v = jnp.dot(flat_prompt, w_value, preferred_element_type=jnp.float32).astype(jnp.bfloat16).reshape(PROBLEMS, PROMPT, width)
    nought = jnp.zeros((), jnp.int32)

    def one_response(carry, index):
        doc_acc, prompt_acc = carry
        index = index.astype(jnp.int32)
        problem = (index % PROBLEMS).astype(jnp.int32)
        pk = lax.dynamic_slice(prompt_k, (problem, nought, nought), (1, PROMPT, width))[0]
        pv = lax.dynamic_slice(prompt_v, (problem, nought, nought), (1, PROMPT, width))[0]
        own_q = lax.dynamic_slice(queries, (index, nought, nought), (1, R, QH * HD))[0]
        own_k = lax.dynamic_slice(resp_keys, (index, nought, nought), (1, R, width))[0]
        own_v = lax.dynamic_slice(resp_values, (index, nought, nought), (1, R, width))[0]
        own_g = lax.dynamic_slice(out_grad, (index, nought, nought), (1, R, QH * HD))[0]
        length = lax.dynamic_slice(lengths, (index,), (1,))[0]
        keys = jnp.concatenate([doc_k, pk, own_k], axis=0)
        values = jnp.concatenate([doc_v, pv, own_v], axis=0)
        rows = jnp.arange(R, dtype=jnp.int32)
        cot = jnp.where((rows < length)[:, None], own_g, jnp.zeros_like(own_g))
        dq, dk, dv = attend(own_q, cot, keys, values, length)
        doc_acc = doc_acc + jnp.stack([dk[:DOC], dv[:DOC]])
        add_on = jnp.stack([dk[DOC:pre], dv[DOC:pre]])[None]
        starts = (problem, nought, nought, nought)
        prompt_acc = lax.dynamic_update_slice(prompt_acc, lax.dynamic_slice(prompt_acc, starts, (1, 2, PROMPT, width)) + add_on, starts)
        return (doc_acc, prompt_acc), (dq, dk[pre:].astype(jnp.bfloat16), dv[pre:].astype(jnp.bfloat16))

    start = (jnp.zeros((2, DOC, width), jnp.float32), jnp.zeros((PROBLEMS, 2, PROMPT, width), jnp.float32))
    (doc_acc, prompt_acc), (grad_queries, grad_keys, grad_values) = lax.scan(one_response, start, jnp.arange(RESPONSES, dtype=jnp.int32))
    doc_sum = doc_acc.astype(jnp.bfloat16)
    prompt_sum = prompt_acc.astype(jnp.bfloat16)
    grad_doc = (jnp.dot(doc_sum[0], w_key.T, preferred_element_type=jnp.float32) + jnp.dot(doc_sum[1], w_value.T, preferred_element_type=jnp.float32)).astype(jnp.bfloat16)
    prompt_keys = prompt_sum[:, 0].reshape(PROBLEMS * PROMPT, width)
    prompt_vals = prompt_sum[:, 1].reshape(PROBLEMS * PROMPT, width)
    grad_prompt = (jnp.dot(prompt_keys, w_key.T, preferred_element_type=jnp.float32) + jnp.dot(prompt_vals, w_value.T, preferred_element_type=jnp.float32)).astype(jnp.bfloat16).reshape(PROBLEMS, PROMPT, D)
    return grad_queries, grad_keys, grad_values, grad_doc, grad_prompt
```

```python
import jax
import jax.numpy as jnp
import numpy as np
from jax import lax
from jax.experimental import pallas as pl
from jax.experimental.pallas import tpu as pltpu
from jax.sharding import PartitionSpec as P

D = 5120
QH = 32
KVH = 4
HD = 128
R = 128
GROUP = QH // KVH
WIDE = GROUP * HD
KVW = 2 * HD
NZ = 4
DOC = 512
PROMPT = 1024
PRE = DOC + PROMPT
KEYS = PRE + R
SCALE = 1.0 / HD**0.5
LOG2E = 1.4426950408889634
MSG = 2 * WIDE + KVW + HD
RET = WIDE + KVW
BF = jnp.bfloat16
F32 = jnp.float32
TILE = 512
VMEM = pl.BlockSpec(memory_space=pltpu.VMEM)
SMEM = pl.BlockSpec(memory_space=pltpu.SMEM)
ANY = pl.BlockSpec(memory_space=pl.ANY)


def part(ref, start, size):
    return ref.at[:, pl.ds(pl.multiple_of(start, 128), size)]


def bundle_copies(q, cot, rk, rv, head, dst, sems, first):
    moves = [
        (part(q.at[0], head * WIDE, WIDE), dst.at[:, pl.ds(0, WIDE)]),
        (part(cot.at[0], head * WIDE, WIDE), dst.at[:, pl.ds(WIDE, WIDE)]),
        (part(rk.at[0], head * HD, HD), dst.at[:, pl.ds(2 * WIDE, HD)]),
        (part(rv.at[0], head * HD, HD), dst.at[:, pl.ds(2 * WIDE + HD, HD)]),
    ]
    return [pltpu.make_async_copy(a, b, sems.at[first + i]) for i, (a, b) in enumerate(moves)]


def live_block(length):
    rows = lax.broadcasted_iota(jnp.int32, (R, HD), 0)
    return jnp.where(rows < length, 1.0, 0.0).astype(BF)


def project_kernel(
    length, pos, xd, xp, wk, wv, q, cot, rk, rv, msg_p, msg_m, msg_2, doc0, doc2, own, acc, live, pair, sems
):
    step = pl.program_id(0)
    y = pos[0]
    heads = [lax.rem(y + 1, 4), lax.rem(y + 3, 4), lax.rem(y + 2, 4)]
    copies = []
    for i, (head, msg) in enumerate(zip(heads, (msg_p, msg_m, msg_2))):
        copies += bundle_copies(q, cot, rk, rv, head, msg, sems, 4 * i)
    for i, msg in enumerate((msg_p, msg_m, msg_2)):
        copies.append(pltpu.make_async_copy(live, msg.at[:, pl.ds(MSG - HD, HD)], sems.at[12 + i]))

    @pl.when(step == 0)
    def _():
        live[...] = live_block(length[0])
        acc[...] = jnp.zeros_like(acc)
        for c in copies:
            c.start()

    x = jnp.concatenate([xd[...], xp[0]], axis=0)
    acc[:, : KVH * HD] += jnp.dot(x, wk[...], preferred_element_type=F32)
    acc[:, KVH * HD :] += jnp.dot(x, wv[...], preferred_element_type=F32)

    @pl.when(step == pl.num_programs(0) - 1)
    def _():
        def head_pair(rows, head):
            at = pl.multiple_of(head * HD, 128)
            return jnp.concatenate(
                [acc[rows, pl.ds(at, HD)], acc[rows, pl.ds(KVH * HD + at, HD)]], axis=1
            ).astype(BF)

        doc_rows, prompt_rows = pl.ds(0, R), pl.ds(R, R)
        pair[0] = head_pair(doc_rows, heads[0])
        pair[1] = head_pair(doc_rows, heads[1])
        extra = [
            pltpu.make_async_copy(pair.at[i], msg.at[:, pl.ds(MSG, KVW)], sems.at[15 + i])
            for i, msg in enumerate((msg_p, msg_m))
        ]
        for c in extra:
            c.start()
        doc2[...] = head_pair(doc_rows, heads[2])
        doc0[...] = head_pair(doc_rows, y)
        own[...] = head_pair(prompt_rows, y)
        for c in copies + extra:
            c.wait()


def project(length, pos, x_doc, x_prompt, w_key, w_value, q, cot, rk, rv):
    out = jax.ShapeDtypeStruct
    return pl.pallas_call(
        project_kernel,
        grid=(D // TILE,),
        out_shape=(
            out((R, MSG + KVW), BF),
            out((R, MSG + KVW), BF),
            out((R, MSG), BF),
            out((R, KVW), BF),
            out((R, KVW), BF),
            out((R, KVW), BF),
        ),
        in_specs=[
            SMEM,
            SMEM,
            pl.BlockSpec((R, TILE), lambda i: (0, i)),
            pl.BlockSpec((1, R, TILE), lambda i: (0, 0, i)),
            pl.BlockSpec((TILE, KVH * HD), lambda i: (i, 0)),
            pl.BlockSpec((TILE, KVH * HD), lambda i: (i, 0)),
            ANY,
            ANY,
            ANY,
            ANY,
        ],
        out_specs=[ANY, ANY, ANY] + [pl.BlockSpec((R, KVW), lambda i: (0, 0))] * 3,
        scratch_shapes=[
            pltpu.VMEM((2 * R, 2 * KVH * HD), F32),
            pltpu.VMEM((R, HD), BF),
            pltpu.VMEM((2, R, KVW), BF),
            pltpu.SemaphoreType.DMA((17,)),
        ],
        compiler_params=pltpu.CompilerParams(vmem_limit_bytes=40 * 2**20),
        cost_estimate=pl.CostEstimate(flops=2 * 256 * D * 1024, bytes_accessed=18 * 2**20, transcendentals=0),
        name="project",
    )(length, pos, x_doc, x_prompt, w_key, w_value, q, cot, rk, rv)


CHUNKS = [(i * 256, 256) for i in range(6)] + [(PRE, R)]


def attend_one(r, msgs, kv, key_t, scores, dprobs, acc, store):
    kv[PRE:, :] = msgs[r, :, 2 * WIDE : 2 * WIDE + KVW]
    key_t[:, PRE:] = kv[PRE:, :HD].T
    live = msgs[r, :, MSG - HD : MSG] > 0
    key_row = lax.broadcasted_iota(jnp.int32, (R, R), 0)
    query_col = lax.broadcasted_iota(jnp.int32, (R, R), 1)
    allowed = (key_row <= query_col) & live
    allowed = jnp.concatenate([allowed, allowed], axis=1)
    acc[PRE:, :] = jnp.zeros((R, KVW), F32)

    def pair(j, carry):
        at = pl.multiple_of(j * KVW, 128)
        two_q = msgs[r, :, pl.ds(at, KVW)]
        two_g = msgs[r, :, pl.ds(pl.multiple_of(WIDE + j * KVW, 128), KVW)]
        nought = jnp.zeros((R, HD), BF)
        q0, q1 = two_q[:, :HD], two_q[:, HD:]
        g0 = jnp.where(live, two_g[:, :HD], nought)
        g1 = jnp.where(live, two_g[:, HD:], nought)
        q_rows = jnp.concatenate([q0, q1], axis=0)
        g_rows = jnp.concatenate([g0, g1], axis=0)
        q_t = jnp.concatenate([q0.T, q1.T], axis=1)
        g_t = jnp.concatenate([g0.T, g1.T], axis=1)
        peak = None
        for start, size in CHUNKS:
            s = jnp.dot(kv[start : start + size, :HD], q_t, preferred_element_type=F32)
            if start == PRE:
                s = jnp.where(allowed, s, -1e30)
            scores[start : start + size, :] = s
            top = jnp.max(s, axis=0, keepdims=True)
            peak = top if peak is None else jnp.maximum(peak, top)
        shift = peak * (SCALE * LOG2E)
        total = jnp.zeros((1, KVW), F32)
        delta = jnp.zeros((1, KVW), F32)
        for start, size in CHUNKS:
            rows = slice(start, start + size)
            e = jnp.exp2(scores[rows, :] * (SCALE * LOG2E) - shift)
            dp = jnp.dot(kv[rows, HD:], g_t, preferred_element_type=F32)
            total += jnp.sum(e, axis=0, keepdims=True)
            delta += jnp.sum(e * dp, axis=0, keepdims=True)
            scores[rows, :] = e
            dprobs[rows, :] = dp
        inv = 1.0 / total
        delta = delta * inv
        dq_t = jnp.zeros((HD, KVW), F32)
        for start, size in CHUNKS:
            rows = slice(start, start + size)
            p = scores[rows, :] * inv
            ds = (p * (dprobs[rows, :] - delta)).astype(BF)
            acc[rows, :HD] += jnp.dot(ds, q_rows, preferred_element_type=F32)
            acc[rows, HD:] += jnp.dot(p.astype(BF), g_rows, preferred_element_type=F32)
            dq_t += jnp.dot(key_t[:, rows], ds, preferred_element_type=F32)
        dq_t = dq_t * SCALE
        store(at, jnp.concatenate([dq_t[:, :HD].T, dq_t[:, HD:].T], axis=1).astype(BF))
        return carry

    lax.fori_loop(0, GROUP // 2, pair, 0)


def scaled(block):
    col = lax.broadcasted_iota(jnp.int32, block.shape, 1)
    return (block * jnp.where(col < HD, SCALE, 1.0)).astype(BF)


def attend_many(count, msgs, kv, key_t, scores, dprobs, acc, rets):
    key_t[:, :PRE] = kv[:PRE, :HD].T

    def response(r, carry):
        def store(at, block):
            rets[r, :, pl.ds(at, KVW)] = block

        attend_one(r, msgs, kv, key_t, scores, dprobs, acc, store)
        rets[r, :, WIDE:] = scaled(acc[PRE:, :])
        return carry

    lax.fori_loop(0, count, response, 0)


def attend_first_kernel(
    length, pos, q, cot, rk, rv, msg_m, msg_p, doc0, doc2, z0, z1, z2, z3,
    ret_0, ret_m, ret_p, kv, acc, msgs, key_t, scores, dprobs, rets, sems,
):
    copies = bundle_copies(q, cot, rk, rv, pos[0], msgs.at[0], sems, 0)
    copies += [
        pltpu.make_async_copy(msg_m, msgs.at[1], sems.at[4]),
        pltpu.make_async_copy(msg_p, msgs.at[2], sems.at[5]),
    ]
    pieces = [doc0, msg_m.at[:, pl.ds(MSG, KVW)], doc2, msg_p.at[:, pl.ds(MSG, KVW)], z0, z1, z2, z3]
    at = 0
    for i, piece in enumerate(pieces):
        rows = R if i < 4 else 2 * R
        copies.append(pltpu.make_async_copy(piece, kv.at[pl.ds(at, rows)], sems.at[6 + i]))
        at += rows
    for c in copies:
        c.start()
    acc[...] = jnp.zeros_like(acc)
    for c in copies:
        c.wait()
    msgs[0, :, MSG - HD : MSG] = live_block(length[0])
    attend_many(3, msgs, kv, key_t, scores, dprobs, acc, rets)
    outs = [
        pltpu.make_async_copy(rets.at[i], out, sems.at[i]) for i, out in enumerate((ret_0, ret_m, ret_p))
    ]
    for c in outs:
        c.start()
    for c in outs:
        c.wait()


def attend_last_kernel(
    pos, msg_2, kv_in, acc_in, ret_2, d0, d1, d2, d3, p0, p1, p2, p3,
    msgs, kv, acc, key_t, scores, dprobs, rets, sems,
):
    copies = [
        pltpu.make_async_copy(msg_2, msgs.at[0], sems.at[0]),
        pltpu.make_async_copy(kv_in, kv, sems.at[1]),
        pltpu.make_async_copy(acc_in, acc, sems.at[2]),
    ]
    for c in copies:
        c.start()
    for c in copies:
        c.wait()
    attend_many(1, msgs, kv, key_t, scores, dprobs, acc, rets)
    ret_2[...] = rets[0]
    for k, out in enumerate((d0, d1, d2, d3)):
        shard = lax.rem(pos[1] + k - pos[0] + 4, 4)
        out[...] = scaled(acc[pl.ds(pl.multiple_of(shard * R, R), R), :])
    for k, out in enumerate((p0, p1, p2, p3)):
        out[...] = scaled(acc[DOC + 2 * R * k : DOC + 2 * R * (k + 1), :])


def work_space(count, width):
    return [pltpu.VMEM((count, R, width), BF)], [
        pltpu.VMEM((HD, KEYS), BF),
        pltpu.VMEM((KEYS, KVW), F32),
        pltpu.VMEM((KEYS, KVW), F32),
        pltpu.VMEM((count, R, RET), BF),
    ]


def attend_cost(count):
    return pl.CostEstimate(
        flops=10 * count * GROUP * R * KEYS * HD * 3, bytes_accessed=2**22, transcendentals=0
    )


def attend_first(length, pos, q, cot, rk, rv, msg_m, msg_p, doc0, doc2, zs):
    out = jax.ShapeDtypeStruct
    head, tail = work_space(3, MSG + KVW)
    return pl.pallas_call(
        attend_first_kernel,
        out_shape=[out((R, RET), BF)] * 3 + [out((KEYS, KVW), BF), out((KEYS, KVW), F32)],
        in_specs=[SMEM, SMEM] + [ANY] * 12,
        out_specs=[ANY] * 3 + [VMEM] * 2,
        scratch_shapes=head + tail + [pltpu.SemaphoreType.DMA((14,))],
        compiler_params=pltpu.CompilerParams(vmem_limit_bytes=40 * 2**20),
        cost_estimate=attend_cost(3),
        name="attend_first",
    )(length, pos, q, cot, rk, rv, msg_m, msg_p, doc0, doc2, *zs)


def attend_last(pos, msg_2, kv, acc):
    out = jax.ShapeDtypeStruct
    head, tail = work_space(1, MSG)
    return pl.pallas_call(
        attend_last_kernel,
        out_shape=[out((R, RET), BF)] + [out((R, KVW), BF)] * 4 + [out((2 * R, KVW), BF)] * 4,
        in_specs=[SMEM] + [ANY] * 3,
        out_specs=[VMEM] * 9,
        scratch_shapes=head
        + [pltpu.VMEM((KEYS, KVW), BF), pltpu.VMEM((KEYS, KVW), F32)]
        + tail
        + [pltpu.SemaphoreType.DMA((3,))],
        compiler_params=pltpu.CompilerParams(vmem_limit_bytes=40 * 2**20),
        cost_estimate=attend_cost(1),
        name="attend_last",
    )(pos, msg_2, kv, acc)


def finish_kernel(
    pos, docs, prompts, wk, wv, r0, r1, r2, r3, grad_doc, grad_prompt, gq, gk, gv, left, sems
):
    step = pl.program_id(0)
    y, z = pos[0], pos[1]
    copies = []
    for k, r in enumerate((r0, r1, r2, r3)):
        head = lax.rem(y + k, 4)
        copies += [
            pltpu.make_async_copy(r.at[:, pl.ds(0, WIDE)], part(gq.at[0], head * WIDE, WIDE), sems.at[3 * k]),
            pltpu.make_async_copy(r.at[:, pl.ds(WIDE, HD)], part(gk.at[0], head * HD, HD), sems.at[3 * k + 1]),
            pltpu.make_async_copy(
                r.at[:, pl.ds(WIDE + HD, HD)], part(gv.at[0], head * HD, HD), sems.at[3 * k + 2]
            ),
        ]

    @pl.when(step == 0)
    def _():
        for c in copies:
            c.start()
        for k in range(4):
            for rows, piece, head in (
                (pl.ds(0, R), docs[k], lax.rem(z + 4 - k, 4)),
                (pl.ds(R, R), prompts[k], lax.rem(y + k, 4)),
            ):
                at = pl.multiple_of(head * HD, 128)
                left[rows, pl.ds(at, HD)] = piece[:, :HD]
                left[rows, pl.ds(KVH * HD + at, HD)] = piece[:, HD:]

    over = (((1,), (1,)), ((), ()))
    total = lax.dot_general(left[:, : KVH * HD], wk[...], over, preferred_element_type=F32)
    total += lax.dot_general(left[:, KVH * HD :], wv[...], over, preferred_element_type=F32)
    grad_doc[...] = total[:R].astype(BF)
    grad_prompt[0] = total[R:].astype(BF)

    @pl.when(step == pl.num_programs(0) - 1)
    def _():
        for c in copies:
            c.wait()


def finish(pos, docs, prompts, w_key, w_value, rets):
    out = jax.ShapeDtypeStruct
    whole = pl.BlockSpec((R, KVW), lambda i: (0, 0))
    weight = pl.BlockSpec((TILE, KVH * HD), lambda i: (i, 0))

    def body(pos, *refs):
        finish_kernel(pos, refs[:4], refs[4:8], *refs[8:])

    return pl.pallas_call(
        body,
        grid=(D // TILE,),
        out_shape=(
            out((R, D), BF),
            out((1, R, D), BF),
            out((1, R, QH * HD), BF),
            out((1, R, KVH * HD), BF),
            out((1, R, KVH * HD), BF),
        ),
        in_specs=[SMEM] + [whole] * 8 + [weight] * 2 + [ANY] * 4,
        out_specs=[
            pl.BlockSpec((R, TILE), lambda i: (0, i)),
            pl.BlockSpec((1, R, TILE), lambda i: (0, 0, i)),
            ANY,
            ANY,
            ANY,
        ],
        scratch_shapes=[pltpu.VMEM((2 * R, 2 * KVH * HD), BF), pltpu.SemaphoreType.DMA((12,))],
        compiler_params=pltpu.CompilerParams(vmem_limit_bytes=40 * 2**20),
        cost_estimate=pl.CostEstimate(flops=2 * 256 * D * 1024, bytes_accessed=18 * 2**20, transcendentals=0),
        name="finish",
    )(pos, *docs, *prompts, w_key, w_value, *rets)


def moves(axes, rule):
    sizes = [lax.axis_size(a) for a in axes]
    pairs = []
    for index in range(np.prod(sizes)):
        here = np.unravel_index(index, sizes)
        there = rule(*(int(i) for i in here))
        pairs.append((index, int(np.ravel_multi_index(there, sizes))))
    return (axes if len(axes) > 1 else axes[0]), pairs


def send(x, move):
    return lax.ppermute(x, *move)


def along_y(k):
    return moves(("doc",), lambda y: ((y + k) % 4,))


def turned(resp, k):
    return ((resp // 2 + k) % NZ) * 2 + resp % 2


def along_z(k):
    return moves(("resp",), lambda r: (turned(r, k),))


def along_x(k):
    def rule(resp, prob):
        x = ((resp % 2) * 2 + prob // 2 + k) % 4
        return (resp // 2) * 2 + x // 2, (x % 2) * 2 + prob % 2

    return moves(("resp", "prob"), rule)


def other_half():
    return moves(("resp",), lambda r: (r ^ 1,))


def other_core():
    return moves(("prob",), lambda p: (p ^ 1,))


def cross(k):
    return moves(("doc", "resp"), lambda y, r: (r // 2, ((y + k) % 4) * 2 + r % 2))


def added(*pieces):
    total = pieces[0].astype(F32)
    for piece in pieces[1:]:
        total = total + piece.astype(F32)
    return total


def on_device(x_doc, x_prompt, w_key, w_value, queries, resp_keys, resp_values, out_grad, lengths):
    y = lax.axis_index("doc")
    z = lax.axis_index("resp") // 2
    pos = jnp.stack([y, z]).astype(jnp.int32)
    msg_p, msg_m, msg_2, doc_0, doc_2, own = project(
        lengths, pos, x_doc, x_prompt, w_key, w_value, queries, out_grad, resp_keys, resp_values
    )
    half = send(own, other_half())
    msg_p = send(msg_p, along_y(1))
    msg_m = send(msg_m, along_y(-1))
    doc_2 = send(doc_2, along_y(2))
    block = jnp.concatenate([own, half], axis=0)
    blocks = [block] + [send(block, along_z(-k)) for k in (1, 2, 3)]
    msg_2 = send(msg_2, along_y(2))
    ret_0, ret_m, ret_p, kv, acc = attend_first(
        lengths, pos, queries, out_grad, resp_keys, resp_values, msg_m, msg_p, doc_0, doc_2, blocks
    )
    ret_2, *terms = attend_last(pos, msg_2, kv, acc)
    doc_terms, prompt_terms = terms[:4], terms[4:]
    doc_got = [doc_terms[0]] + [send(doc_terms[k], along_z(k)) for k in (1, 2, 3)]
    prompt_got = [prompt_terms[0]] + [send(prompt_terms[k], along_z(k)) for k in (1, 2, 3)]
    doc = added(*doc_got).astype(BF)
    doc = added(doc, send(doc, other_core())).astype(BF)
    doc = added(doc, *(send(doc, along_x(k)) for k in (1, 2, 3))).astype(BF)
    docs = [send(doc, cross(k)) for k in range(4)]
    prompt = added(*prompt_got)
    prompt = (prompt[:R] + send(prompt[R:].astype(BF), other_half()).astype(F32)).astype(BF)
    prompts = [prompt] + [send(prompt, along_y(-k)) for k in (1, 2, 3)]
    rets = [ret_0, send(ret_p, along_y(-1)), send(ret_2, along_y(2)), send(ret_m, along_y(1))]
    grad_doc, grad_prompt, gq, gk, gv = finish(pos, docs, prompts, w_key, w_value, rets)
    return gq, gk, gv, grad_doc, grad_prompt


def solution(mesh):
    placed = (
        P("doc", None),
        P("prob", "resp", None),
        P(),
        P(),
        P(("doc", "resp", "prob"), None, None),
        P(("doc", "resp", "prob"), None, None),
        P(("doc", "resp", "prob"), None, None),
        P(("doc", "resp", "prob"), None, None),
        P(("doc", "resp", "prob")),
    )
    return jax.shard_map(
        on_device,
        mesh=mesh,
        in_specs=placed,
        out_specs=(
            P(("doc", "resp", "prob"), None, None),
            P(("doc", "resp", "prob"), None, None),
            P(("doc", "resp", "prob"), None, None),
            P("doc", None),
            P("prob", "resp", None),
        ),
        check_vma=False,
    )
```

```python
import jax
import jax.numpy as jnp
import numpy as np
from jax import lax
from jax.experimental import pallas as pl
from jax.experimental.pallas import tpu as pltpu
from jax.sharding import PartitionSpec as P

D = 5120
QH = 32
KVH = 4
HD = 128
R = 128
GROUP = QH // KVH
WIDE = GROUP * HD
KVW = 2 * HD
NZ = 4
DOC = 512
PROMPT = 1024
PRE = DOC + PROMPT
KEYS = PRE + R
SCALE = 1.0 / HD**0.5
LOG2E = 1.4426950408889634
MSG = 2 * WIDE + KVW + HD
RET = WIDE + KVW
BF = jnp.bfloat16
F32 = jnp.float32
TILE = 1024
VMEM = pl.BlockSpec(memory_space=pltpu.VMEM)
SMEM = pl.BlockSpec(memory_space=pltpu.SMEM)
ANY = pl.BlockSpec(memory_space=pl.ANY)


def live_block(length):
    rows = lax.broadcasted_iota(jnp.int32, (R, HD), 0)
    return jnp.where(rows < length, 1.0, 0.0).astype(BF)


def project_kernel(
    length, xd, xp, wk, wv, q, cot, rk, rv, msg_p, msg_m, msg_2, doc_0, doc_1, doc_2, own,
    xs, ws, qs, gs, ks, vs, acc, sems,
):
    y = lax.axis_index("doc")
    first = [
        pltpu.make_async_copy(xd, xs.at[pl.ds(0, R)], sems.at[0]),
        pltpu.make_async_copy(xp.at[0], xs.at[pl.ds(R, R)], sems.at[1]),
    ]
    parts = []
    for i in range(D // TILE):
        rows = pl.ds(i * TILE, TILE)
        parts.append(
            [
                pltpu.make_async_copy(wk.at[rows], ws.at[0, rows], sems.at[6 + 2 * i]),
                pltpu.make_async_copy(wv.at[rows], ws.at[1, rows], sems.at[7 + 2 * i]),
            ]
        )
    rest = [
        pltpu.make_async_copy(a.at[0], b, sems.at[2 + i])
        for i, (a, b) in enumerate(((q, qs), (cot, gs), (rk, ks), (rv, vs)))
    ]
    for c in first + sum(parts, []) + rest:
        c.start()
    for c in first:
        c.wait()
    for i, part_copies in enumerate(parts):
        for c in part_copies:
            c.wait()
        rows = slice(i * TILE, (i + 1) * TILE)
        x = xs[:, rows]
        for k in range(2):
            cols = slice(k * KVH * HD, (k + 1) * KVH * HD)
            term = jnp.dot(x, ws[k, rows, :], preferred_element_type=F32)
            acc[:, cols] = term if i == 0 else acc[:, cols] + term

    def head_pair(row, head):
        at = pl.multiple_of(head * HD, 128)
        return jnp.concatenate(
            [acc[row : row + R, pl.ds(at, HD)], acc[row : row + R, pl.ds(KVH * HD + at, HD)]], axis=1
        ).astype(BF)

    own[...] = head_pair(R, y)
    core = lax.rem(lax.axis_index("prob"), 2)
    for step, doc in ((0, doc_0), (1 + 2 * core, doc_1), (2, doc_2)):
        doc[...] = head_pair(0, lax.rem(y + step, 4))
    for c in rest:
        c.wait()
    live = live_block(length[0])
    for step, msg in ((1, msg_p), (3, msg_m), (2, msg_2)):
        head = lax.rem(y + step, 4)
        wide = pl.ds(pl.multiple_of(head * WIDE, 128), WIDE)
        thin = pl.ds(pl.multiple_of(head * HD, 128), HD)
        msg[:, :WIDE] = qs[:, wide]
        msg[:, WIDE : 2 * WIDE] = gs[:, wide]
        msg[:, 2 * WIDE : 2 * WIDE + HD] = ks[:, thin]
        msg[:, 2 * WIDE + HD : 2 * WIDE + KVW] = vs[:, thin]
        msg[:, MSG - HD : MSG] = live


def project(length, x_doc, x_prompt, w_key, w_value, q, cot, rk, rv):
    out = jax.ShapeDtypeStruct
    return pl.pallas_call(
        project_kernel,
        out_shape=(
            out((R, MSG), BF),
            out((R, MSG), BF),
            out((R, MSG), BF),
            out((R, KVW), BF),
            out((R, KVW), BF),
            out((R, KVW), BF),
            out((R, KVW), BF),
        ),
        in_specs=[SMEM] + [ANY] * 8,
        out_specs=[VMEM] * 7,
        scratch_shapes=[
            pltpu.VMEM((2 * R, D), BF),
            pltpu.VMEM((2, D, KVH * HD), BF),
            pltpu.VMEM((R, QH * HD), BF),
            pltpu.VMEM((R, QH * HD), BF),
            pltpu.VMEM((R, KVH * HD), BF),
            pltpu.VMEM((R, KVH * HD), BF),
            pltpu.VMEM((2 * R, 2 * KVH * HD), F32),
            pltpu.SemaphoreType.DMA((6 + 2 * (D // TILE),)),
        ],
        compiler_params=pltpu.CompilerParams(vmem_limit_bytes=56 * 2**20),
        cost_estimate=pl.CostEstimate(flops=2 * 256 * D * 1024, bytes_accessed=18 * 2**20, transcendentals=0),
        name="project",
    )(length, x_doc, x_prompt, w_key, w_value, q, cot, rk, rv)


CHUNK = 256
FIRST_COST = 5 * 10**9
MID_COST = 10**10
LAST_COST = 5 * 10**9


def attend_one(q_of, g_of, own, live, kv, key_t, before, acc, own_acc, ret, scores, dprobs):
    own_t = own[:, :HD].T
    key_row = lax.broadcasted_iota(jnp.int32, (R, R), 0)
    query_col = lax.broadcasted_iota(jnp.int32, (R, R), 1)
    allowed = (key_row <= query_col) & live
    allowed = jnp.concatenate([allowed, allowed], axis=1)
    chunks = [(i, CHUNK) for i in range(0, PRE, CHUNK)] + [(PRE, R)]

    def keys_of(start, size):
        return own[:, :HD] if start == PRE else kv[start : start + size, :HD]

    def values_of(start, size):
        return own[:, HD:] if start == PRE else kv[start : start + size, HD:]

    for j in range(GROUP // 2):
        two_q, two_g = q_of(j), g_of(j)
        nought = jnp.zeros((R, HD), BF)
        q0, q1 = two_q[:, :HD], two_q[:, HD:]
        g0 = jnp.where(live, two_g[:, :HD], nought)
        g1 = jnp.where(live, two_g[:, HD:], nought)
        q_rows = jnp.concatenate([q0, q1], axis=0)
        g_rows = jnp.concatenate([g0, g1], axis=0)
        q_t = jnp.concatenate([q0.T, q1.T], axis=1)
        g_t = jnp.concatenate([g0.T, g1.T], axis=1)
        peak = None
        for start, size in chunks:
            s = jnp.dot(keys_of(start, size), q_t, preferred_element_type=F32)
            if start == PRE:
                s = jnp.where(allowed, s, -1e30)
            scores[start : start + size, :] = s
            top = jnp.max(s, axis=0, keepdims=True)
            peak = top if peak is None else jnp.maximum(peak, top)
        shift = peak * (SCALE * LOG2E)
        total = jnp.zeros((1, KVW), F32)
        delta = jnp.zeros((1, KVW), F32)
        for start, size in chunks:
            rows = slice(start, start + size)
            e = jnp.exp2(scores[rows, :] * (SCALE * LOG2E) - shift)
            dp = jnp.dot(values_of(start, size), g_t, preferred_element_type=F32)
            total += jnp.sum(e, axis=0, keepdims=True)
            delta += jnp.sum(e * dp, axis=0, keepdims=True)
            scores[rows, :] = e
            dprobs[rows, :] = dp
        inv = 1.0 / total
        delta = delta * inv
        dq_t = jnp.zeros((HD, KVW), F32)
        for start, size in chunks:
            rows = slice(start, start + size)
            p = scores[rows, :] * inv
            ds = (p * (dprobs[rows, :] - delta)).astype(BF)
            dk = jnp.dot(ds, q_rows, preferred_element_type=F32)
            dv = jnp.dot(p.astype(BF), g_rows, preferred_element_type=F32)
            if start == PRE:
                where, old = own_acc, own_acc if j else None
                rows = slice(0, R)
                left = own_t
            else:
                where, old = acc, acc if j else before
                left = key_t[:, rows]
            where[rows, :HD] = dk if old is None else old[rows, :HD] + dk
            where[rows, HD:] = dv if old is None else old[rows, HD:] + dv
            dq_t += jnp.dot(left, ds, preferred_element_type=F32)
        dq_t = dq_t * SCALE
        ret[:, j * KVW : (j + 1) * KVW] = jnp.concatenate([dq_t[:, :HD].T, dq_t[:, HD:].T], axis=1).astype(BF)
    ret[:, WIDE:] = scaled(own_acc[...])


def scaled(block):
    col = lax.broadcasted_iota(jnp.int32, block.shape, 1)
    return (block * jnp.where(col < HD, SCALE, 1.0)).astype(BF)


def attend_bundle(msg, *rest):
    def q_of(j):
        return msg[:, j * KVW : (j + 1) * KVW]

    def g_of(j):
        return msg[:, WIDE + j * KVW : WIDE + (j + 1) * KVW]

    own = msg[:, 2 * WIDE : 2 * WIDE + KVW]
    attend_one(q_of, g_of, own, msg[:, MSG - HD :] > 0, *rest)


def attend_first_kernel(
    length, q, cot, rk, rv, doc_0, mine, other, doc_2, z0, z1, z2, z3,
    ret, kv, key_t, acc, own_acc, scores, dprobs,
):
    core = lax.rem(lax.axis_index("prob"), 2)
    for row, piece in ((0, doc_0), (3 - 2 * core, mine), (1 + 2 * core, other), (2, doc_2)):
        kv[pl.ds(pl.multiple_of(row * R, R), R), :] = piece[...]
    for k, block in enumerate((z0, z1, z2, z3)):
        kv[DOC + 2 * R * k : DOC + 2 * R * (k + 1), :] = block[...]
    key_t[...] = kv[:, :HD].T
    head = lax.axis_index("doc")

    def q_of(j):
        return q[0, :, pl.ds(pl.multiple_of(head * WIDE + j * KVW, 128), KVW)]

    def g_of(j):
        return cot[0, :, pl.ds(pl.multiple_of(head * WIDE + j * KVW, 128), KVW)]

    thin = pl.ds(pl.multiple_of(head * HD, 128), HD)
    own = jnp.concatenate([rk[0, :, thin], rv[0, :, thin]], axis=1)
    live = live_block(length[0]) > 0
    attend_one(q_of, g_of, own, live, kv, key_t, None, acc, own_acc, ret, scores, dprobs)


def attend_mid_kernel(msg_m, msg_p, kv, key_t, before, ret_m, ret_p, acc, own_acc, scores, dprobs):
    attend_bundle(msg_m, kv, key_t, before, acc, own_acc, ret_m, scores, dprobs)
    attend_bundle(msg_p, kv, key_t, acc, acc, own_acc, ret_p, scores, dprobs)


def attend_last_kernel(msg_2, kv, key_t, before, ret_2, m0, m1, m2, m3, acc, own_acc, scores, dprobs):
    attend_bundle(msg_2, kv, key_t, before, acc, own_acc, ret_2, scores, dprobs)
    y, z = lax.axis_index("doc"), lax.axis_index("resp") // 2
    for k, out in enumerate((m0, m1, m2, m3)):
        rows = pl.ds(pl.multiple_of(lax.rem(z + k - y + 4, 4) * R, R), R)
        out[:R] = scaled(acc[rows, :])
        out[R:] = scaled(acc[DOC + 2 * R * k : DOC + 2 * R * (k + 1), :])


RET_SHAPE = jax.ShapeDtypeStruct((R, RET), BF)
ACC_SHAPE = jax.ShapeDtypeStruct((PRE, KVW), F32)


def attend(kernel, name, count, in_specs, outs, scratch, *args):
    return pl.pallas_call(
        kernel,
        out_shape=outs,
        in_specs=in_specs,
        out_specs=[VMEM] * len(outs),
        scratch_shapes=scratch
        + [pltpu.VMEM((R, KVW), F32), pltpu.VMEM((KEYS, KVW), F32), pltpu.VMEM((KEYS, KVW), F32)],
        compiler_params=pltpu.CompilerParams(vmem_limit_bytes=24 * 2**20),
        cost_estimate=pl.CostEstimate(
            flops=count, bytes_accessed=0, transcendentals=0
        ),
        name=name,
    )(*args)


def attend_first(length, q, cot, rk, rv, docs, zs):
    out = jax.ShapeDtypeStruct
    outs = [RET_SHAPE, out((PRE, KVW), BF), out((HD, PRE), BF), ACC_SHAPE]
    specs = [SMEM] + [VMEM] * 12
    return attend(attend_first_kernel, "attend_first", FIRST_COST, specs, outs, [], length, q, cot, rk, rv, *docs, *zs)


def attend_mid(msg_m, msg_p, kv, key_t, acc):
    outs = [RET_SHAPE, RET_SHAPE, ACC_SHAPE]
    return attend(attend_mid_kernel, "attend_mid", MID_COST, [VMEM] * 5, outs, [], msg_m, msg_p, kv, key_t, acc)


def attend_last(msg_2, kv, key_t, acc):
    outs = [RET_SHAPE] + [jax.ShapeDtypeStruct((3 * R, KVW), BF)] * 4
    scratch = [pltpu.VMEM((PRE, KVW), F32)]
    return attend(attend_last_kernel, "attend_last", LAST_COST, [VMEM] * 4, outs, scratch, msg_2, kv, key_t, acc)


def unpack_kernel(r0, r1, r2, r3, gq, gk, gv):
    for k, r in enumerate((r0, r1, r2, r3)):
        head = lax.rem(lax.axis_index("doc") + k, 4)
        thin = pl.ds(pl.multiple_of(head * HD, 128), HD)
        gq[0, :, pl.ds(pl.multiple_of(head * WIDE, 128), WIDE)] = r[:, :WIDE]
        gk[0, :, thin] = r[:, WIDE : WIDE + HD]
        gv[0, :, thin] = r[:, WIDE + HD :]


def unpack(rets):
    out = jax.ShapeDtypeStruct
    return pl.pallas_call(
        unpack_kernel,
        out_shape=(out((1, R, QH * HD), BF), out((1, R, KVH * HD), BF), out((1, R, KVH * HD), BF)),
        in_specs=[VMEM] * 4,
        out_specs=[VMEM] * 3,
        compiler_params=pltpu.CompilerParams(vmem_limit_bytes=12 * 2**20),
        cost_estimate=pl.CostEstimate(flops=0, bytes_accessed=2**22, transcendentals=0),
        name="unpack",
    )(*rets)


def finish_kernel(d0, d1, d2, d3, p0, p1, p2, p3, wk, wv, grad_doc, grad_prompt, left, out, sems):
    y, z, core = lax.axis_index("doc"), lax.axis_index("resp") // 2, lax.axis_index("prob") % 2
    for k, (doc, prompt) in enumerate(((d0, p0), (d1, p1), (d2, p2), (d3, p3))):
        step = lax.rem(2 * core + k, 4)
        for row, piece, head in ((0, doc, lax.rem(z + 4 - step, 4)), (R, prompt, lax.rem(y + k, 4))):
            at = pl.multiple_of(head * HD, 128)
            left[row : row + R, pl.ds(at, HD)] = piece[:, :HD]
            left[row : row + R, pl.ds(KVH * HD + at, HD)] = piece[:, HD:]
    over = (((1,), (1,)), ((), ()))
    copies = []
    for i in range(D // TILE):
        cols = slice(i * TILE, (i + 1) * TILE)
        total = lax.dot_general(left[:, : KVH * HD], wk[cols, :], over, preferred_element_type=F32)
        total += lax.dot_general(left[:, KVH * HD :], wv[cols, :], over, preferred_element_type=F32)
        out[:, cols] = total.astype(BF)
        cols = pl.ds(i * TILE, TILE)
        copies += [
            pltpu.make_async_copy(out.at[pl.ds(0, R), cols], grad_doc.at[:, cols], sems.at[2 * i]),
            pltpu.make_async_copy(out.at[pl.ds(R, R), cols], grad_prompt.at[0, :, cols], sems.at[2 * i + 1]),
        ]
        copies[-2].start()
        copies[-1].start()
    for c in copies:
        c.wait()


def finish(docs, prompts, w_key, w_value):
    out = jax.ShapeDtypeStruct
    return pl.pallas_call(
        finish_kernel,
        out_shape=(out((R, D), BF), out((1, R, D), BF)),
        in_specs=[VMEM] * 10,
        out_specs=[ANY, ANY],
        scratch_shapes=[
            pltpu.VMEM((2 * R, 2 * KVH * HD), BF),
            pltpu.VMEM((2 * R, D), BF),
            pltpu.SemaphoreType.DMA((2 * (D // TILE),)),
        ],
        compiler_params=pltpu.CompilerParams(vmem_limit_bytes=20 * 2**20),
        cost_estimate=pl.CostEstimate(flops=2 * 256 * D * 1024, bytes_accessed=18 * 2**20, transcendentals=0),
        name="finish",
    )(*docs, *prompts, w_key, w_value)


def moves(axes, rule):
    sizes = [lax.axis_size(a) for a in axes]
    pairs = []
    for index in range(np.prod(sizes)):
        here = np.unravel_index(index, sizes)
        there = rule(*(int(i) for i in here))
        pairs.append((index, int(np.ravel_multi_index(there, sizes))))
    return (axes if len(axes) > 1 else axes[0]), pairs


def send(x, move):
    return lax.ppermute(x, *move)


def along_y(k):
    return moves(("doc",), lambda y: ((y + k) % 4,))


def turned(resp, k):
    return ((resp // 2 + k) % NZ) * 2 + resp % 2


def beside_y():
    return moves(("doc", "prob"), lambda y, p: ((y + 1 + 2 * (p % 2)) % 4, p))


def along_z(k):
    return moves(("resp",), lambda r: (turned(r, k),))


def along_x(k):
    def rule(resp, prob):
        x = ((resp % 2) * 2 + prob // 2 + k) % 4
        return (resp // 2) * 2 + x // 2, (x % 2) * 2 + prob % 2

    return moves(("resp", "prob"), rule)


def other_half():
    return moves(("resp",), lambda r: (r ^ 1,))


def other_core():
    return moves(("prob",), lambda p: (p ^ 1,))


def cross(first, second):
    def rule(y, resp, prob):
        k = first if prob % 2 == 0 else second
        return resp // 2, ((y + k) % 4) * 2 + resp % 2, prob

    return moves(("doc", "resp", "prob"), rule)


def added(*pieces):
    total = pieces[0].astype(F32)
    for piece in pieces[1:]:
        total = total + piece.astype(F32)
    return total


def sum_kernel(m0, m1, m2, m3, doc, keep, give):
    total = added(m0[...], m1[...], m2[...], m3[...])
    doc[...] = total[:R].astype(BF)
    keep[...] = total[R : 2 * R]
    give[...] = total[2 * R :].astype(BF)


def sum_blocks(blocks):
    out = jax.ShapeDtypeStruct
    return pl.pallas_call(
        sum_kernel,
        out_shape=(out((R, KVW), BF), out((R, KVW), F32), out((R, KVW), BF)),
        in_specs=[VMEM] * 4,
        out_specs=[VMEM] * 3,
        compiler_params=pltpu.CompilerParams(vmem_limit_bytes=8 * 2**20),
        cost_estimate=pl.CostEstimate(flops=2**18, bytes_accessed=2**20, transcendentals=0),
        name="sum_blocks",
    )(*blocks)


def on_device(x_doc, x_prompt, w_key, w_value, queries, resp_keys, resp_values, out_grad, lengths):
    msg_p, msg_m, msg_2, doc_0, doc_1, doc_2, own = project(
        lengths, x_doc, x_prompt, w_key, w_value, queries, out_grad, resp_keys, resp_values
    )
    half = send(own, other_half())
    doc_1 = send(doc_1, beside_y())
    doc_2 = send(doc_2, along_y(2))
    half, doc_2 = lax.optimization_barrier((half, doc_2))
    docs = [doc_0, doc_1, send(doc_1, other_core()), doc_2]
    block = jnp.concatenate([own, half], axis=0)
    blocks = [block] + [send(block, along_z(-k)) for k in (1, 2, 3)]
    msg_p = send(msg_p, along_y(1))
    msg_m = send(msg_m, along_y(-1))
    msg_2 = send(msg_2, along_y(2))
    ret_0, kv, key_t, acc = attend_first(
        lengths, queries, out_grad, resp_keys, resp_values, docs, blocks
    )
    ret_m, ret_p, acc = attend_mid(msg_m, msg_p, kv, key_t, acc)
    ret_1 = send(ret_p, along_y(-1))
    ret_3 = send(ret_m, along_y(1))
    ret_2, *terms = attend_last(msg_2, kv, key_t, acc)
    terms, ret_1, ret_3 = lax.optimization_barrier((terms, ret_1, ret_3))
    ret_2 = send(ret_2, along_y(2))
    doc, keep, give = sum_blocks([terms[0]] + [send(terms[k], along_z(k)) for k in (1, 2, 3)])
    doc = added(doc, send(doc, other_core())).astype(BF)
    doc = added(doc, *(send(doc, along_x(k)) for k in (1, 2, 3))).astype(BF)
    prompt = added(keep, send(give, other_half())).astype(BF)
    doc, ret_2 = lax.optimization_barrier((doc, ret_2))
    mine = [send(doc, cross(0, 2)), send(doc, cross(1, 3))]
    docs = mine + [send(piece, other_core()) for piece in mine]
    prompts = [prompt] + [send(prompt, along_y(-k)) for k in (1, 2, 3)]
    gq, gk, gv = unpack([ret_0, ret_1, ret_2, ret_3])
    grad_doc, grad_prompt = finish(docs, prompts, w_key, w_value)
    return gq, gk, gv, grad_doc, grad_prompt


def solution(mesh):
    placed = (
        P("doc", None),
        P("prob", "resp", None),
        P(),
        P(),
        P(("doc", "resp", "prob"), None, None),
        P(("doc", "resp", "prob"), None, None),
        P(("doc", "resp", "prob"), None, None),
        P(("doc", "resp", "prob"), None, None),
        P(("doc", "resp", "prob")),
    )
    return jax.shard_map(
        on_device,
        mesh=mesh,
        in_specs=placed,
        out_specs=(
            P(("doc", "resp", "prob"), None, None),
            P(("doc", "resp", "prob"), None, None),
            P(("doc", "resp", "prob"), None, None),
            P("doc", None),
            P("prob", "resp", None),
        ),
        check_vma=False,
    )
```

```python
import jax
import jax.numpy as jnp
import numpy as np
from jax import lax
from jax.experimental import pallas as pl
from jax.experimental.pallas import tpu as pltpu
from jax.sharding import PartitionSpec as P

D = 5120
QH = 32
KVH = 4
HD = 128
R = 128
GROUP = QH // KVH
WIDE = GROUP * HD
KVW = 2 * HD
NZ = 4
DOC = 512
PROMPT = 1024
PRE = DOC + PROMPT
KEYS = PRE + R
SCALE = 1.0 / HD**0.5
LOG2E = 1.4426950408889634
MSG = 2 * WIDE + KVW + HD
RET = WIDE + KVW
BF = jnp.bfloat16
F32 = jnp.float32
TILE = 1024
VMEM = pl.BlockSpec(memory_space=pltpu.VMEM)
SMEM = pl.BlockSpec(memory_space=pltpu.SMEM)
ANY = pl.BlockSpec(memory_space=pl.ANY)


def live_block(length):
    rows = lax.broadcasted_iota(jnp.int32, (R, HD), 0)
    return jnp.where(rows < length, 1.0, 0.0).astype(BF)


def project_kernel(
    length, xd, xp, wk, wv, q, cot, rk, rv, msg_p, msg_m, msg_2, doc_0, doc_1, doc_2, own,
    xs, ws, qs, gs, ks, vs, acc, sems,
):
    y = lax.axis_index("doc")
    first = [
        pltpu.make_async_copy(xd, xs.at[pl.ds(0, R)], sems.at[0]),
        pltpu.make_async_copy(xp.at[0], xs.at[pl.ds(R, R)], sems.at[1]),
    ]
    parts = []
    for i in range(D // TILE):
        rows = pl.ds(i * TILE, TILE)
        parts.append(
            [
                pltpu.make_async_copy(wk.at[rows], ws.at[0, rows], sems.at[6 + 2 * i]),
                pltpu.make_async_copy(wv.at[rows], ws.at[1, rows], sems.at[7 + 2 * i]),
            ]
        )
    rest = [
        pltpu.make_async_copy(a.at[0], b, sems.at[2 + i])
        for i, (a, b) in enumerate(((q, qs), (cot, gs), (rk, ks), (rv, vs)))
    ]
    for c in first + sum(parts, []) + rest:
        c.start()
    for c in first:
        c.wait()
    for i, part_copies in enumerate(parts):
        for c in part_copies:
            c.wait()
        rows = slice(i * TILE, (i + 1) * TILE)
        x = xs[:, rows]
        for k in range(2):
            cols = slice(k * KVH * HD, (k + 1) * KVH * HD)
            term = jnp.dot(x, ws[k, rows, :], preferred_element_type=F32)
            acc[:, cols] = term if i == 0 else acc[:, cols] + term

    def head_pair(row, head):
        at = pl.multiple_of(head * HD, 128)
        return jnp.concatenate(
            [acc[row : row + R, pl.ds(at, HD)], acc[row : row + R, pl.ds(KVH * HD + at, HD)]], axis=1
        ).astype(BF)

    own[...] = head_pair(R, y)
    core = lax.rem(lax.axis_index("prob"), 2)
    for step, doc in ((0, doc_0), (1 + 2 * core, doc_1), (2, doc_2)):
        doc[...] = head_pair(0, lax.rem(y + step, 4))
    for c in rest:
        c.wait()
    live = live_block(length[0])
    for step, msg in ((1, msg_p), (3, msg_m), (2, msg_2)):
        head = lax.rem(y + step, 4)
        wide = pl.ds(pl.multiple_of(head * WIDE, 128), WIDE)
        thin = pl.ds(pl.multiple_of(head * HD, 128), HD)
        msg[:, :WIDE] = qs[:, wide]
        msg[:, WIDE : 2 * WIDE] = gs[:, wide]
        msg[:, 2 * WIDE : 2 * WIDE + HD] = ks[:, thin]
        msg[:, 2 * WIDE + HD : 2 * WIDE + KVW] = vs[:, thin]
        msg[:, MSG - HD : MSG] = live


def project(length, x_doc, x_prompt, w_key, w_value, q, cot, rk, rv):
    out = jax.ShapeDtypeStruct
    return pl.pallas_call(
        project_kernel,
        out_shape=(
            out((R, MSG), BF),
            out((R, MSG), BF),
            out((R, MSG), BF),
            out((R, KVW), BF),
            out((R, KVW), BF),
            out((R, KVW), BF),
            out((R, KVW), BF),
        ),
        in_specs=[SMEM] + [ANY] * 8,
        out_specs=[VMEM] * 7,
        scratch_shapes=[
            pltpu.VMEM((2 * R, D), BF),
            pltpu.VMEM((2, D, KVH * HD), BF),
            pltpu.VMEM((R, QH * HD), BF),
            pltpu.VMEM((R, QH * HD), BF),
            pltpu.VMEM((R, KVH * HD), BF),
            pltpu.VMEM((R, KVH * HD), BF),
            pltpu.VMEM((2 * R, 2 * KVH * HD), F32),
            pltpu.SemaphoreType.DMA((6 + 2 * (D // TILE),)),
        ],
        compiler_params=pltpu.CompilerParams(vmem_limit_bytes=56 * 2**20),
        cost_estimate=pl.CostEstimate(flops=2 * 256 * D * 1024, bytes_accessed=18 * 2**20, transcendentals=0),
        name="project",
    )(length, x_doc, x_prompt, w_key, w_value, q, cot, rk, rv)


CHUNK = 256
FIRST_COST = 5 * 10**9
MID_COST = 10**10
LAST_COST = 5 * 10**9


def attend_one(q_of, g_of, own, live, kv, key_t, before, acc, own_acc, ret, scores, dprobs):
    own_t = own[:, :HD].T
    key_row = lax.broadcasted_iota(jnp.int32, (R, R), 0)
    query_col = lax.broadcasted_iota(jnp.int32, (R, R), 1)
    allowed = (key_row <= query_col) & live
    allowed = jnp.concatenate([allowed, allowed], axis=1)
    chunks = [(i, CHUNK) for i in range(0, PRE, CHUNK)] + [(PRE, R)]

    def keys_of(start, size):
        return own[:, :HD] if start == PRE else kv[start : start + size, :HD]

    def values_of(start, size):
        return own[:, HD:] if start == PRE else kv[start : start + size, HD:]

    state = {}

    def prepare(j):
        two_q, two_g = q_of(j), g_of(j)
        nought = jnp.zeros((R, HD), BF)
        q0, q1 = two_q[:, :HD], two_q[:, HD:]
        g0 = jnp.where(live, two_g[:, :HD], nought)
        g1 = jnp.where(live, two_g[:, HD:], nought)
        state[j] = dict(
            q_rows=jnp.concatenate([q0, q1], axis=0),
            g_rows=jnp.concatenate([g0, g1], axis=0),
            q_t=jnp.concatenate([q0.T, q1.T], axis=1),
            g_t=jnp.concatenate([g0.T, g1.T], axis=1),
            peak=None,
            total=jnp.zeros((1, KVW), F32),
            delta=jnp.zeros((1, KVW), F32),
            dq_t=jnp.zeros((HD, KVW), F32),
        )

    def step_a(j, start, size):
        st = state[j]
        s = jnp.dot(keys_of(start, size), st["q_t"], preferred_element_type=F32)
        if start == PRE:
            s = jnp.where(allowed, s, -1e30)
        scores[j % 2, start : start + size, :] = s
        top = jnp.max(s, axis=0, keepdims=True)
        st["peak"] = top if st["peak"] is None else jnp.maximum(st["peak"], top)

    def step_b(j, start, size):
        st = state[j]
        rows = slice(start, start + size)
        e = jnp.exp2(scores[j % 2, rows, :] * (SCALE * LOG2E) - st["shift"])
        dp = jnp.dot(values_of(start, size), st["g_t"], preferred_element_type=F32)
        st["total"] += jnp.sum(e, axis=0, keepdims=True)
        st["delta"] += jnp.sum(e * dp, axis=0, keepdims=True)
        scores[j % 2, rows, :] = e
        dprobs[j % 2, rows, :] = dp

    def step_c(j, start, size):
        st = state[j]
        rows = slice(start, start + size)
        p = scores[j % 2, rows, :] * st["inv"]
        ds = (p * (dprobs[j % 2, rows, :] - st["delta"])).astype(BF)
        dk = jnp.dot(ds, st["q_rows"], preferred_element_type=F32)
        dv = jnp.dot(p.astype(BF), st["g_rows"], preferred_element_type=F32)
        if start == PRE:
            where, old = own_acc, own_acc if j else None
            rows = slice(0, R)
            left = own_t
        else:
            where, old = acc, acc if j else before
            left = key_t[:, rows]
        where[rows, :HD] = dk if old is None else old[rows, :HD] + dk
        where[rows, HD:] = dv if old is None else old[rows, HD:] + dv
        st["dq_t"] += jnp.dot(left, ds, preferred_element_type=F32)

    def end_a(j):
        state[j]["shift"] = state[j]["peak"] * (SCALE * LOG2E)

    def end_b(j):
        state[j]["inv"] = 1.0 / state[j]["total"]
        state[j]["delta"] = state[j]["delta"] * state[j]["inv"]

    def end_c(j):
        dq_t = state[j]["dq_t"] * SCALE
        ret[:, j * KVW : (j + 1) * KVW] = jnp.concatenate([dq_t[:, :HD].T, dq_t[:, HD:].T], axis=1).astype(BF)

    last = GROUP // 2 - 1
    prepare(0)
    for c in chunks:
        step_a(0, *c)
    end_a(0)
    for j in range(GROUP // 2):
        if j < last:
            prepare(j + 1)
        for c in chunks:
            step_b(j, *c)
            if j < last:
                step_a(j + 1, *c)
        end_b(j)
        if j < last:
            end_a(j + 1)
        for c in chunks:
            step_c(j, *c)
        end_c(j)
    ret[:, WIDE:] = scaled(own_acc[...])


def scaled(block):
    col = lax.broadcasted_iota(jnp.int32, block.shape, 1)
    return (block * jnp.where(col < HD, SCALE, 1.0)).astype(BF)


def attend_bundle(msg, *rest):
    def q_of(j):
        return msg[:, j * KVW : (j + 1) * KVW]

    def g_of(j):
        return msg[:, WIDE + j * KVW : WIDE + (j + 1) * KVW]

    own = msg[:, 2 * WIDE : 2 * WIDE + KVW]
    attend_one(q_of, g_of, own, msg[:, MSG - HD :] > 0, *rest)


def attend_first_kernel(
    length, q, cot, rk, rv, doc_0, mine, other, doc_2, z0, z1, z2, z3,
    ret, kv, key_t, acc, own_acc, scores, dprobs,
):
    core = lax.rem(lax.axis_index("prob"), 2)
    for row, piece in ((0, doc_0), (3 - 2 * core, mine), (1 + 2 * core, other), (2, doc_2)):
        kv[pl.ds(pl.multiple_of(row * R, R), R), :] = piece[...]
    for k, block in enumerate((z0, z1, z2, z3)):
        kv[DOC + 2 * R * k : DOC + 2 * R * (k + 1), :] = block[...]
    key_t[...] = kv[:, :HD].T
    head = lax.axis_index("doc")

    def q_of(j):
        return q[0, :, pl.ds(pl.multiple_of(head * WIDE + j * KVW, 128), KVW)]

    def g_of(j):
        return cot[0, :, pl.ds(pl.multiple_of(head * WIDE + j * KVW, 128), KVW)]

    thin = pl.ds(pl.multiple_of(head * HD, 128), HD)
    own = jnp.concatenate([rk[0, :, thin], rv[0, :, thin]], axis=1)
    live = live_block(length[0]) > 0
    attend_one(q_of, g_of, own, live, kv, key_t, None, acc, own_acc, ret, scores, dprobs)


def attend_mid_kernel(msg_m, msg_p, kv, key_t, before, ret_m, ret_p, acc, own_acc, scores, dprobs):
    attend_bundle(msg_m, kv, key_t, before, acc, own_acc, ret_m, scores, dprobs)
    attend_bundle(msg_p, kv, key_t, acc, acc, own_acc, ret_p, scores, dprobs)


def attend_last_kernel(msg_2, kv, key_t, before, ret_2, m0, m1, m2, m3, acc, own_acc, scores, dprobs):
    attend_bundle(msg_2, kv, key_t, before, acc, own_acc, ret_2, scores, dprobs)
    y, z = lax.axis_index("doc"), lax.axis_index("resp") // 2
    for k, out in enumerate((m0, m1, m2, m3)):
        rows = pl.ds(pl.multiple_of(lax.rem(z + k - y + 4, 4) * R, R), R)
        out[:R] = scaled(acc[rows, :])
        out[R:] = scaled(acc[DOC + 2 * R * k : DOC + 2 * R * (k + 1), :])


RET_SHAPE = jax.ShapeDtypeStruct((R, RET), BF)
ACC_SHAPE = jax.ShapeDtypeStruct((PRE, KVW), F32)


def attend(kernel, name, count, in_specs, outs, scratch, *args):
    return pl.pallas_call(
        kernel,
        out_shape=outs,
        in_specs=in_specs,
        out_specs=[VMEM] * len(outs),
        scratch_shapes=scratch
        + [pltpu.VMEM((R, KVW), F32), pltpu.VMEM((2, KEYS, KVW), F32), pltpu.VMEM((2, KEYS, KVW), F32)],
        compiler_params=pltpu.CompilerParams(vmem_limit_bytes=24 * 2**20),
        cost_estimate=pl.CostEstimate(
            flops=count, bytes_accessed=0, transcendentals=0
        ),
        name=name,
    )(*args)


def attend_first(length, q, cot, rk, rv, docs, zs):
    out = jax.ShapeDtypeStruct
    outs = [RET_SHAPE, out((PRE, KVW), BF), out((HD, PRE), BF), ACC_SHAPE]
    specs = [SMEM] + [VMEM] * 12
    return attend(attend_first_kernel, "attend_first", FIRST_COST, specs, outs, [], length, q, cot, rk, rv, *docs, *zs)


def attend_mid(msg_m, msg_p, kv, key_t, acc):
    outs = [RET_SHAPE, RET_SHAPE, ACC_SHAPE]
    return attend(attend_mid_kernel, "attend_mid", MID_COST, [VMEM] * 5, outs, [], msg_m, msg_p, kv, key_t, acc)


def attend_last(msg_2, kv, key_t, acc):
    outs = [RET_SHAPE] + [jax.ShapeDtypeStruct((3 * R, KVW), BF)] * 4
    scratch = [pltpu.VMEM((PRE, KVW), F32)]
    return attend(attend_last_kernel, "attend_last", LAST_COST, [VMEM] * 4, outs, scratch, msg_2, kv, key_t, acc)


def unpack_kernel(r0, r1, r2, r3, gq, gk, gv):
    for k, r in enumerate((r0, r1, r2, r3)):
        head = lax.rem(lax.axis_index("doc") + k, 4)
        thin = pl.ds(pl.multiple_of(head * HD, 128), HD)
        gq[0, :, pl.ds(pl.multiple_of(head * WIDE, 128), WIDE)] = r[:, :WIDE]
        gk[0, :, thin] = r[:, WIDE : WIDE + HD]
        gv[0, :, thin] = r[:, WIDE + HD :]


def unpack(rets):
    out = jax.ShapeDtypeStruct
    return pl.pallas_call(
        unpack_kernel,
        out_shape=(out((1, R, QH * HD), BF), out((1, R, KVH * HD), BF), out((1, R, KVH * HD), BF)),
        in_specs=[VMEM] * 4,
        out_specs=[VMEM] * 3,
        compiler_params=pltpu.CompilerParams(vmem_limit_bytes=12 * 2**20),
        cost_estimate=pl.CostEstimate(flops=0, bytes_accessed=2**22, transcendentals=0),
        name="unpack",
    )(*rets)


def finish_kernel(d0, d1, d2, d3, p0, p1, p2, p3, wk, wv, grad_doc, grad_prompt, left, out, sems):
    y, z, core = lax.axis_index("doc"), lax.axis_index("resp") // 2, lax.axis_index("prob") % 2
    for k, (doc, prompt) in enumerate(((d0, p0), (d1, p1), (d2, p2), (d3, p3))):
        step = lax.rem(2 * core + k, 4)
        for row, piece, head in ((0, doc, lax.rem(z + 4 - step, 4)), (R, prompt, lax.rem(y + k, 4))):
            at = pl.multiple_of(head * HD, 128)
            left[row : row + R, pl.ds(at, HD)] = piece[:, :HD]
            left[row : row + R, pl.ds(KVH * HD + at, HD)] = piece[:, HD:]
    over = (((1,), (1,)), ((), ()))
    copies = []
    for i in range(D // TILE):
        cols = slice(i * TILE, (i + 1) * TILE)
        total = lax.dot_general(left[:, : KVH * HD], wk[cols, :], over, preferred_element_type=F32)
        total += lax.dot_general(left[:, KVH * HD :], wv[cols, :], over, preferred_element_type=F32)
        out[:, cols] = total.astype(BF)
        cols = pl.ds(i * TILE, TILE)
        copies += [
            pltpu.make_async_copy(out.at[pl.ds(0, R), cols], grad_doc.at[:, cols], sems.at[2 * i]),
            pltpu.make_async_copy(out.at[pl.ds(R, R), cols], grad_prompt.at[0, :, cols], sems.at[2 * i + 1]),
        ]
        copies[-2].start()
        copies[-1].start()
    for c in copies:
        c.wait()


def finish(docs, prompts, w_key, w_value):
    out = jax.ShapeDtypeStruct
    return pl.pallas_call(
        finish_kernel,
        out_shape=(out((R, D), BF), out((1, R, D), BF)),
        in_specs=[VMEM] * 10,
        out_specs=[ANY, ANY],
        scratch_shapes=[
            pltpu.VMEM((2 * R, 2 * KVH * HD), BF),
            pltpu.VMEM((2 * R, D), BF),
            pltpu.SemaphoreType.DMA((2 * (D // TILE),)),
        ],
        compiler_params=pltpu.CompilerParams(vmem_limit_bytes=20 * 2**20),
        cost_estimate=pl.CostEstimate(flops=2 * 256 * D * 1024, bytes_accessed=18 * 2**20, transcendentals=0),
        name="finish",
    )(*docs, *prompts, w_key, w_value)


def moves(axes, rule):
    sizes = [lax.axis_size(a) for a in axes]
    pairs = []
    for index in range(np.prod(sizes)):
        here = np.unravel_index(index, sizes)
        there = rule(*(int(i) for i in here))
        pairs.append((index, int(np.ravel_multi_index(there, sizes))))
    return (axes if len(axes) > 1 else axes[0]), pairs


def send(x, move):
    return lax.ppermute(x, *move)


def along_y(k):
    return moves(("doc",), lambda y: ((y + k) % 4,))


def turned(resp, k):
    return ((resp // 2 + k) % NZ) * 2 + resp % 2


def beside_y():
    return moves(("doc", "prob"), lambda y, p: ((y + 1 + 2 * (p % 2)) % 4, p))


def along_z(k):
    return moves(("resp",), lambda r: (turned(r, k),))


def along_x(k):
    def rule(resp, prob):
        x = ((resp % 2) * 2 + prob // 2 + k) % 4
        return (resp // 2) * 2 + x // 2, (x % 2) * 2 + prob % 2

    return moves(("resp", "prob"), rule)


def other_half():
    return moves(("resp",), lambda r: (r ^ 1,))


def other_core():
    return moves(("prob",), lambda p: (p ^ 1,))


def cross(first, second):
    def rule(y, resp, prob):
        k = first if prob % 2 == 0 else second
        return resp // 2, ((y + k) % 4) * 2 + resp % 2, prob

    return moves(("doc", "resp", "prob"), rule)


def added(*pieces):
    total = pieces[0].astype(F32)
    for piece in pieces[1:]:
        total = total + piece.astype(F32)
    return total


def sum_kernel(m0, m1, m2, m3, doc, keep, give):
    total = added(m0[...], m1[...], m2[...], m3[...])
    doc[...] = total[:R].astype(BF)
    keep[...] = total[R : 2 * R]
    give[...] = total[2 * R :].astype(BF)


def sum_blocks(blocks):
    out = jax.ShapeDtypeStruct
    return pl.pallas_call(
        sum_kernel,
        out_shape=(out((R, KVW), BF), out((R, KVW), F32), out((R, KVW), BF)),
        in_specs=[VMEM] * 4,
        out_specs=[VMEM] * 3,
        compiler_params=pltpu.CompilerParams(vmem_limit_bytes=8 * 2**20),
        cost_estimate=pl.CostEstimate(flops=2**18, bytes_accessed=2**20, transcendentals=0),
        name="sum_blocks",
    )(*blocks)


def on_device(x_doc, x_prompt, w_key, w_value, queries, resp_keys, resp_values, out_grad, lengths):
    msg_p, msg_m, msg_2, doc_0, doc_1, doc_2, own = project(
        lengths, x_doc, x_prompt, w_key, w_value, queries, out_grad, resp_keys, resp_values
    )
    half = send(own, other_half())
    doc_1 = send(doc_1, beside_y())
    doc_2 = send(doc_2, along_y(2))
    half, doc_2 = lax.optimization_barrier((half, doc_2))
    docs = [doc_0, doc_1, send(doc_1, other_core()), doc_2]
    block = jnp.concatenate([own, half], axis=0)
    blocks = [block] + [send(block, along_z(-k)) for k in (1, 2, 3)]
    msg_p = send(msg_p, along_y(1))
    msg_m = send(msg_m, along_y(-1))
    msg_2 = send(msg_2, along_y(2))
    ret_0, kv, key_t, acc = attend_first(
        lengths, queries, out_grad, resp_keys, resp_values, docs, blocks
    )
    ret_m, ret_p, acc = attend_mid(msg_m, msg_p, kv, key_t, acc)
    ret_1 = send(ret_p, along_y(-1))
    ret_3 = send(ret_m, along_y(1))
    ret_2, *terms = attend_last(msg_2, kv, key_t, acc)
    ret_2 = send(ret_2, along_y(2))
    blocks = [terms[0]] + [send(terms[k], along_z(k)) for k in (1, 2, 3)]
    blocks, ret_1, ret_3 = lax.optimization_barrier((blocks, ret_1, ret_3))
    doc, keep, give = sum_blocks(blocks)
    doc = added(doc, send(doc, other_core())).astype(BF)
    doc = added(doc, *(send(doc, along_x(k)) for k in (1, 2, 3))).astype(BF)
    prompt = added(keep, send(give, other_half())).astype(BF)
    doc, ret_2 = lax.optimization_barrier((doc, ret_2))
    mine = [send(doc, cross(0, 2)), send(doc, cross(1, 3))]
    docs = mine + [send(piece, other_core()) for piece in mine]
    prompts = [prompt] + [send(prompt, along_y(-k)) for k in (1, 2, 3)]
    gq, gk, gv = unpack([ret_0, ret_1, ret_2, ret_3])
    grad_doc, grad_prompt = finish(docs, prompts, w_key, w_value)
    return gq, gk, gv, grad_doc, grad_prompt


def solution(mesh):
    placed = (
        P("doc", None),
        P("prob", "resp", None),
        P(),
        P(),
        P(("doc", "resp", "prob"), None, None),
        P(("doc", "resp", "prob"), None, None),
        P(("doc", "resp", "prob"), None, None),
        P(("doc", "resp", "prob"), None, None),
        P(("doc", "resp", "prob")),
    )
    return jax.shard_map(
        on_device,
        mesh=mesh,
        in_specs=placed,
        out_specs=(
            P(("doc", "resp", "prob"), None, None),
            P(("doc", "resp", "prob"), None, None),
            P(("doc", "resp", "prob"), None, None),
            P("doc", None),
            P("prob", "resp", None),
        ),
        check_vma=False,
    )
```

```python
import jax
import jax.numpy as jnp
import numpy as np
from jax import lax
from jax.experimental import pallas as pl
from jax.experimental.pallas import tpu as pltpu
from jax.sharding import PartitionSpec as P

D = 5120
QH = 32
KVH = 4
HD = 128
R = 128
GROUP = QH // KVH
WIDE = GROUP * HD
KVW = 2 * HD
NZ = 4
DOC = 512
PROMPT = 1024
PRE = DOC + PROMPT
KEYS = PRE + R
SCALE = 1.0 / HD**0.5
LOG2E = 1.4426950408889634
MSG = 2 * WIDE + KVW + HD
RET = WIDE + KVW
BF = jnp.bfloat16
F32 = jnp.float32
TILE = 1024
VMEM = pl.BlockSpec(memory_space=pltpu.VMEM)
SMEM = pl.BlockSpec(memory_space=pltpu.SMEM)
ANY = pl.BlockSpec(memory_space=pl.ANY)


def live_block(length):
    rows = lax.broadcasted_iota(jnp.int32, (R, HD), 0)
    return jnp.where(rows < length, 1.0, 0.0).astype(BF)


def project_kernel(
    length, xd, xp, wk, wv, q, cot, rk, rv, msg_p, msg_m, msg_2, doc_0, doc_1, doc_2, own,
    xs, ws, qs, gs, ks, vs, acc, sems,
):
    y = lax.axis_index("doc")
    first = [
        pltpu.make_async_copy(xd, xs.at[pl.ds(0, R)], sems.at[0]),
        pltpu.make_async_copy(xp.at[0], xs.at[pl.ds(R, R)], sems.at[1]),
    ]
    parts = []
    for i in range(D // TILE):
        rows = pl.ds(i * TILE, TILE)
        parts.append(
            [
                pltpu.make_async_copy(wk.at[rows], ws.at[0, rows], sems.at[6 + 2 * i]),
                pltpu.make_async_copy(wv.at[rows], ws.at[1, rows], sems.at[7 + 2 * i]),
            ]
        )
    rest = [
        pltpu.make_async_copy(a.at[0], b, sems.at[2 + i])
        for i, (a, b) in enumerate(((q, qs), (cot, gs), (rk, ks), (rv, vs)))
    ]
    for c in first + sum(parts, []) + rest:
        c.start()
    for c in first:
        c.wait()
    for i, part_copies in enumerate(parts):
        for c in part_copies:
            c.wait()
        rows = slice(i * TILE, (i + 1) * TILE)
        x = xs[:, rows]
        for k in range(2):
            cols = slice(k * KVH * HD, (k + 1) * KVH * HD)
            term = jnp.dot(x, ws[k, rows, :], preferred_element_type=F32)
            acc[:, cols] = term if i == 0 else acc[:, cols] + term

    def head_pair(row, head):
        at = pl.multiple_of(head * HD, 128)
        return jnp.concatenate(
            [acc[row : row + R, pl.ds(at, HD)], acc[row : row + R, pl.ds(KVH * HD + at, HD)]], axis=1
        ).astype(BF)

    own[...] = head_pair(R, y)
    core = lax.rem(lax.axis_index("prob"), 2)
    for step, doc in ((0, doc_0), (1 + 2 * core, doc_1), (2, doc_2)):
        doc[...] = head_pair(0, lax.rem(y + step, 4))
    for c in rest:
        c.wait()
    live = live_block(length[0])
    for step, msg in ((1, msg_p), (3, msg_m), (2, msg_2)):
        head = lax.rem(y + step, 4)
        wide = pl.ds(pl.multiple_of(head * WIDE, 128), WIDE)
        thin = pl.ds(pl.multiple_of(head * HD, 128), HD)
        msg[:, :WIDE] = qs[:, wide]
        msg[:, WIDE : 2 * WIDE] = gs[:, wide]
        msg[:, 2 * WIDE : 2 * WIDE + HD] = ks[:, thin]
        msg[:, 2 * WIDE + HD : 2 * WIDE + KVW] = vs[:, thin]
        msg[:, MSG - HD : MSG] = live


def project(length, x_doc, x_prompt, w_key, w_value, q, cot, rk, rv):
    out = jax.ShapeDtypeStruct
    return pl.pallas_call(
        project_kernel,
        out_shape=(
            out((R, MSG), BF),
            out((R, MSG), BF),
            out((R, MSG), BF),
            out((R, KVW), BF),
            out((R, KVW), BF),
            out((R, KVW), BF),
            out((R, KVW), BF),
        ),
        in_specs=[SMEM] + [ANY] * 8,
        out_specs=[VMEM] * 7,
        scratch_shapes=[
            pltpu.VMEM((2 * R, D), BF),
            pltpu.VMEM((2, D, KVH * HD), BF),
            pltpu.VMEM((R, QH * HD), BF),
            pltpu.VMEM((R, QH * HD), BF),
            pltpu.VMEM((R, KVH * HD), BF),
            pltpu.VMEM((R, KVH * HD), BF),
            pltpu.VMEM((2 * R, 2 * KVH * HD), F32),
            pltpu.SemaphoreType.DMA((6 + 2 * (D // TILE),)),
        ],
        compiler_params=pltpu.CompilerParams(vmem_limit_bytes=56 * 2**20),
        cost_estimate=pl.CostEstimate(flops=2 * 256 * D * 1024, bytes_accessed=18 * 2**20, transcendentals=0),
        name="project",
    )(length, x_doc, x_prompt, w_key, w_value, q, cot, rk, rv)


CHUNK = 256
FIRST_COST = 5 * 10**9
MID_COST = 10**10
LAST_COST = 5 * 10**9


def attend_some(responses, kv, key_t, before, acc, own_acc, scores, dprobs):
    key_row = lax.broadcasted_iota(jnp.int32, (R, R), 0)
    query_col = lax.broadcasted_iota(jnp.int32, (R, R), 1)
    chunks = [(i, CHUNK) for i in range(0, PRE, CHUNK)] + [(PRE, R)]
    pairs = GROUP // 2
    items = [(r, j) for r in range(len(responses)) for j in range(pairs)]
    state = {}

    def prepare(i):
        r, j = items[i]
        q_of, g_of, own, live, ret = responses[r]
        if j == 0:
            allowed = (key_row <= query_col) & live
            state["own", r] = own, own[:, :HD].T, jnp.concatenate([allowed, allowed], axis=1)
        two_q, two_g = q_of(j), g_of(j)
        nought = jnp.zeros((R, HD), BF)
        q0, q1 = two_q[:, :HD], two_q[:, HD:]
        g0 = jnp.where(live, two_g[:, :HD], nought)
        g1 = jnp.where(live, two_g[:, HD:], nought)
        state[i] = dict(
            q_rows=jnp.concatenate([q0, q1], axis=0),
            g_rows=jnp.concatenate([g0, g1], axis=0),
            q_t=jnp.concatenate([q0.T, q1.T], axis=1),
            g_t=jnp.concatenate([g0.T, g1.T], axis=1),
            peak=None,
            total=jnp.zeros((1, KVW), F32),
            delta=jnp.zeros((1, KVW), F32),
            dq_t=jnp.zeros((HD, KVW), F32),
        )

    def step_a(i, start, size):
        st = state[i]
        own, _, allowed = state["own", items[i][0]]
        keys = own[:, :HD] if start == PRE else kv[start : start + size, :HD]
        s = jnp.dot(keys, st["q_t"], preferred_element_type=F32)
        if start == PRE:
            s = jnp.where(allowed, s, -1e30)
        scores[i % 2, start : start + size, :] = s
        top = jnp.max(s, axis=0, keepdims=True)
        st["peak"] = top if st["peak"] is None else jnp.maximum(st["peak"], top)

    def end_a(i):
        state[i]["shift"] = state[i]["peak"] * (SCALE * LOG2E)

    def step_b(i, start, size):
        st = state[i]
        rows = slice(start, start + size)
        values = state["own", items[i][0]][0][:, HD:] if start == PRE else kv[rows, HD:]
        e = jnp.exp2(scores[i % 2, rows, :] * (SCALE * LOG2E) - st["shift"])
        dp = jnp.dot(values, st["g_t"], preferred_element_type=F32)
        st["total"] += jnp.sum(e, axis=0, keepdims=True)
        st["delta"] += jnp.sum(e * dp, axis=0, keepdims=True)
        scores[i % 2, rows, :] = e
        dprobs[i % 2, rows, :] = dp

    def end_b(i):
        state[i]["inv"] = 1.0 / state[i]["total"]
        state[i]["delta"] = state[i]["delta"] * state[i]["inv"]

    def step_c(i, start, size):
        st = state[i]
        r, j = items[i]
        rows = slice(start, start + size)
        p = scores[i % 2, rows, :] * st["inv"]
        ds = (p * (dprobs[i % 2, rows, :] - st["delta"])).astype(BF)
        dk = jnp.dot(ds, st["q_rows"], preferred_element_type=F32)
        dv = jnp.dot(p.astype(BF), st["g_rows"], preferred_element_type=F32)
        if start == PRE:
            where, old = own_acc, own_acc if j else None
            rows = slice(0, R)
            left = state["own", r][1]
        else:
            where, old = acc, acc if i else before
            left = key_t[:, rows]
        where[rows, :HD] = dk if old is None else old[rows, :HD] + dk
        where[rows, HD:] = dv if old is None else old[rows, HD:] + dv
        st["dq_t"] += jnp.dot(left, ds, preferred_element_type=F32)

    def end_c(i):
        r, j = items[i]
        ret = responses[r][4]
        dq_t = state[i]["dq_t"] * SCALE
        ret[:, j * KVW : (j + 1) * KVW] = jnp.concatenate([dq_t[:, :HD].T, dq_t[:, HD:].T], axis=1).astype(BF)
        if j == pairs - 1:
            ret[:, WIDE:] = scaled(own_acc[...])

    n = len(items)
    for i in range(-1, n):
        if i + 1 < n:
            prepare(i + 1)
        for c in chunks:
            if i >= 0:
                step_b(i, *c)
            if i + 1 < n:
                step_a(i + 1, *c)
        if i + 1 < n:
            end_a(i + 1)
        if i >= 0:
            end_b(i)
            for c in chunks:
                step_c(i, *c)
            end_c(i)


def scaled(block):
    col = lax.broadcasted_iota(jnp.int32, block.shape, 1)
    return (block * jnp.where(col < HD, SCALE, 1.0)).astype(BF)


def bundled(msg, ret):
    def q_of(j):
        return msg[:, j * KVW : (j + 1) * KVW]

    def g_of(j):
        return msg[:, WIDE + j * KVW : WIDE + (j + 1) * KVW]

    return q_of, g_of, msg[:, 2 * WIDE : 2 * WIDE + KVW], msg[:, MSG - HD :] > 0, ret


def attend_first_kernel(
    length, q, cot, rk, rv, doc_0, mine, other, doc_2, z0, z1, z2, z3,
    ret, kv, key_t, acc, own_acc, scores, dprobs,
):
    core = lax.rem(lax.axis_index("prob"), 2)
    for row, piece in ((0, doc_0), (3 - 2 * core, mine), (1 + 2 * core, other), (2, doc_2)):
        kv[pl.ds(pl.multiple_of(row * R, R), R), :] = piece[...]
    for k, block in enumerate((z0, z1, z2, z3)):
        kv[DOC + 2 * R * k : DOC + 2 * R * (k + 1), :] = block[...]
    key_t[...] = kv[:, :HD].T
    head = lax.axis_index("doc")

    def q_of(j):
        return q[0, :, pl.ds(pl.multiple_of(head * WIDE + j * KVW, 128), KVW)]

    def g_of(j):
        return cot[0, :, pl.ds(pl.multiple_of(head * WIDE + j * KVW, 128), KVW)]

    thin = pl.ds(pl.multiple_of(head * HD, 128), HD)
    own = jnp.concatenate([rk[0, :, thin], rv[0, :, thin]], axis=1)
    live = live_block(length[0]) > 0
    attend_some([(q_of, g_of, own, live, ret)], kv, key_t, None, acc, own_acc, scores, dprobs)


def attend_mid_kernel(msg_m, msg_p, kv, key_t, before, ret_m, ret_p, acc, ret, own_acc, scores, dprobs):
    acc[...] = before[...]

    def response(r, carry):
        def either(start, size):
            cols = slice(start, start + size)
            return jnp.where(r == 0, msg_m[:, cols], msg_p[:, cols])

        def q_of(j):
            return either(j * KVW, KVW)

        def g_of(j):
            return either(WIDE + j * KVW, KVW)

        live = either(MSG - HD, HD) > 0
        one = q_of, g_of, either(2 * WIDE, KVW), live, ret
        attend_some([one], kv, key_t, acc, acc, own_acc, scores, dprobs)

        @pl.when(r == 0)
        def _():
            ret_m[...] = ret[...]

        @pl.when(r == 1)
        def _():
            ret_p[...] = ret[...]

        return carry

    lax.fori_loop(0, 2, response, 0)


def attend_last_kernel(msg_2, kv, key_t, before, ret_2, m0, m1, m2, m3, acc, own_acc, scores, dprobs):
    attend_some([bundled(msg_2, ret_2)], kv, key_t, before, acc, own_acc, scores, dprobs)
    y, z = lax.axis_index("doc"), lax.axis_index("resp") // 2
    for k, out in enumerate((m0, m1, m2, m3)):
        rows = pl.ds(pl.multiple_of(lax.rem(z + k - y + 4, 4) * R, R), R)
        out[:R] = scaled(acc[rows, :])
        out[R:] = scaled(acc[DOC + 2 * R * k : DOC + 2 * R * (k + 1), :])


RET_SHAPE = jax.ShapeDtypeStruct((R, RET), BF)
ACC_SHAPE = jax.ShapeDtypeStruct((PRE, KVW), F32)


def attend(kernel, name, count, in_specs, outs, scratch, *args):
    return pl.pallas_call(
        kernel,
        out_shape=outs,
        in_specs=in_specs,
        out_specs=[VMEM] * len(outs),
        scratch_shapes=scratch
        + [pltpu.VMEM((R, KVW), F32), pltpu.VMEM((2, KEYS, KVW), F32), pltpu.VMEM((2, KEYS, KVW), F32)],
        compiler_params=pltpu.CompilerParams(vmem_limit_bytes=24 * 2**20),
        cost_estimate=pl.CostEstimate(
            flops=count, bytes_accessed=0, transcendentals=0
        ),
        name=name,
    )(*args)


def attend_first(length, q, cot, rk, rv, docs, zs):
    out = jax.ShapeDtypeStruct
    outs = [RET_SHAPE, out((PRE, KVW), BF), out((HD, PRE), BF), ACC_SHAPE]
    specs = [SMEM] + [VMEM] * 12
    return attend(attend_first_kernel, "attend_first", FIRST_COST, specs, outs, [], length, q, cot, rk, rv, *docs, *zs)


def attend_mid(msg_m, msg_p, kv, key_t, acc):
    outs = [RET_SHAPE, RET_SHAPE, ACC_SHAPE]
    scratch = [pltpu.VMEM((R, RET), BF)]
    return attend(attend_mid_kernel, "attend_mid", MID_COST, [VMEM] * 5, outs, scratch, msg_m, msg_p, kv, key_t, acc)


def attend_last(msg_2, kv, key_t, acc):
    outs = [RET_SHAPE] + [jax.ShapeDtypeStruct((3 * R, KVW), BF)] * 4
    scratch = [pltpu.VMEM((PRE, KVW), F32)]
    return attend(attend_last_kernel, "attend_last", LAST_COST, [VMEM] * 4, outs, scratch, msg_2, kv, key_t, acc)


def unpack_kernel(r0, r1, r2, r3, gq, gk, gv):
    for k, r in enumerate((r0, r1, r2, r3)):
        head = lax.rem(lax.axis_index("doc") + k, 4)
        thin = pl.ds(pl.multiple_of(head * HD, 128), HD)
        gq[0, :, pl.ds(pl.multiple_of(head * WIDE, 128), WIDE)] = r[:, :WIDE]
        gk[0, :, thin] = r[:, WIDE : WIDE + HD]
        gv[0, :, thin] = r[:, WIDE + HD :]


def unpack(rets):
    out = jax.ShapeDtypeStruct
    return pl.pallas_call(
        unpack_kernel,
        out_shape=(out((1, R, QH * HD), BF), out((1, R, KVH * HD), BF), out((1, R, KVH * HD), BF)),
        in_specs=[VMEM] * 4,
        out_specs=[VMEM] * 3,
        compiler_params=pltpu.CompilerParams(vmem_limit_bytes=12 * 2**20),
        cost_estimate=pl.CostEstimate(flops=0, bytes_accessed=2**22, transcendentals=0),
        name="unpack",
    )(*rets)


def finish_kernel(d0, d1, d2, d3, p0, p1, p2, p3, wk, wv, grad_doc, grad_prompt, left, out, sems):
    y, z, core = lax.axis_index("doc"), lax.axis_index("resp") // 2, lax.axis_index("prob") % 2
    for k, (doc, prompt) in enumerate(((d0, p0), (d1, p1), (d2, p2), (d3, p3))):
        step = lax.rem(2 * core + k, 4)
        for row, piece, head in ((0, doc, lax.rem(z + 4 - step, 4)), (R, prompt, lax.rem(y + k, 4))):
            at = pl.multiple_of(head * HD, 128)
            left[row : row + R, pl.ds(at, HD)] = piece[:, :HD]
            left[row : row + R, pl.ds(KVH * HD + at, HD)] = piece[:, HD:]
    over = (((1,), (1,)), ((), ()))
    copies = []
    for i in range(D // TILE):
        cols = slice(i * TILE, (i + 1) * TILE)
        total = lax.dot_general(left[:, : KVH * HD], wk[cols, :], over, preferred_element_type=F32)
        total += lax.dot_general(left[:, KVH * HD :], wv[cols, :], over, preferred_element_type=F32)
        out[:, cols] = total.astype(BF)
        cols = pl.ds(i * TILE, TILE)
        copies += [
            pltpu.make_async_copy(out.at[pl.ds(0, R), cols], grad_doc.at[:, cols], sems.at[2 * i]),
            pltpu.make_async_copy(out.at[pl.ds(R, R), cols], grad_prompt.at[0, :, cols], sems.at[2 * i + 1]),
        ]
        copies[-2].start()
        copies[-1].start()
    for c in copies:
        c.wait()


def finish(docs, prompts, w_key, w_value):
    out = jax.ShapeDtypeStruct
    return pl.pallas_call(
        finish_kernel,
        out_shape=(out((R, D), BF), out((1, R, D), BF)),
        in_specs=[VMEM] * 10,
        out_specs=[ANY, ANY],
        scratch_shapes=[
            pltpu.VMEM((2 * R, 2 * KVH * HD), BF),
            pltpu.VMEM((2 * R, D), BF),
            pltpu.SemaphoreType.DMA((2 * (D // TILE),)),
        ],
        compiler_params=pltpu.CompilerParams(vmem_limit_bytes=20 * 2**20),
        cost_estimate=pl.CostEstimate(flops=2 * 256 * D * 1024, bytes_accessed=18 * 2**20, transcendentals=0),
        name="finish",
    )(*docs, *prompts, w_key, w_value)


def moves(axes, rule):
    sizes = [lax.axis_size(a) for a in axes]
    pairs = []
    for index in range(np.prod(sizes)):
        here = np.unravel_index(index, sizes)
        there = rule(*(int(i) for i in here))
        pairs.append((index, int(np.ravel_multi_index(there, sizes))))
    return (axes if len(axes) > 1 else axes[0]), pairs


def send(x, move):
    return lax.ppermute(x, *move)


def along_y(k):
    return moves(("doc",), lambda y: ((y + k) % 4,))


def turned(resp, k):
    return ((resp // 2 + k) % NZ) * 2 + resp % 2


def beside_y():
    return moves(("doc", "prob"), lambda y, p: ((y + 1 + 2 * (p % 2)) % 4, p))


def along_z(k):
    return moves(("resp",), lambda r: (turned(r, k),))


def along_x(k):
    def rule(resp, prob):
        x = ((resp % 2) * 2 + prob // 2 + k) % 4
        return (resp // 2) * 2 + x // 2, (x % 2) * 2 + prob % 2

    return moves(("resp", "prob"), rule)


def other_half():
    return moves(("resp",), lambda r: (r ^ 1,))


def other_core():
    return moves(("prob",), lambda p: (p ^ 1,))


def cross(first, second):
    def rule(y, resp, prob):
        k = first if prob % 2 == 0 else second
        return resp // 2, ((y + k) % 4) * 2 + resp % 2, prob

    return moves(("doc", "resp", "prob"), rule)


def added(*pieces):
    total = pieces[0].astype(F32)
    for piece in pieces[1:]:
        total = total + piece.astype(F32)
    return total


def sum_kernel(m0, m1, m2, m3, doc, keep, give):
    total = added(m0[...], m1[...], m2[...], m3[...])
    doc[...] = total[:R].astype(BF)
    keep[...] = total[R : 2 * R]
    give[...] = total[2 * R :].astype(BF)


def sum_blocks(blocks):
    out = jax.ShapeDtypeStruct
    return pl.pallas_call(
        sum_kernel,
        out_shape=(out((R, KVW), BF), out((R, KVW), F32), out((R, KVW), BF)),
        in_specs=[VMEM] * 4,
        out_specs=[VMEM] * 3,
        compiler_params=pltpu.CompilerParams(vmem_limit_bytes=8 * 2**20),
        cost_estimate=pl.CostEstimate(flops=2**18, bytes_accessed=2**20, transcendentals=0),
        name="sum_blocks",
    )(*blocks)


def on_device(x_doc, x_prompt, w_key, w_value, queries, resp_keys, resp_values, out_grad, lengths):
    msg_p, msg_m, msg_2, doc_0, doc_1, doc_2, own = project(
        lengths, x_doc, x_prompt, w_key, w_value, queries, out_grad, resp_keys, resp_values
    )
    half = send(own, other_half())
    doc_1 = send(doc_1, beside_y())
    doc_2 = send(doc_2, along_y(2))
    half, doc_2 = lax.optimization_barrier((half, doc_2))
    docs = [doc_0, doc_1, send(doc_1, other_core()), doc_2]
    block = jnp.concatenate([own, half], axis=0)
    blocks = [block] + [send(block, along_z(-k)) for k in (1, 2, 3)]
    msg_p = send(msg_p, along_y(1))
    msg_m = send(msg_m, along_y(-1))
    msg_2 = send(msg_2, along_y(2))
    ret_0, kv, key_t, acc = attend_first(
        lengths, queries, out_grad, resp_keys, resp_values, docs, blocks
    )
    ret_m, ret_p, acc = attend_mid(msg_m, msg_p, kv, key_t, acc)
    ret_1 = send(ret_p, along_y(-1))
    ret_3 = send(ret_m, along_y(1))
    ret_2, *terms = attend_last(msg_2, kv, key_t, acc)
    ret_2 = send(ret_2, along_y(2))
    blocks = [terms[0]] + [send(terms[k], along_z(k)) for k in (1, 2, 3)]
    blocks, ret_1, ret_3 = lax.optimization_barrier((blocks, ret_1, ret_3))
    doc, keep, give = sum_blocks(blocks)
    doc = added(doc, send(doc, other_core())).astype(BF)
    doc = added(doc, *(send(doc, along_x(k)) for k in (1, 2, 3))).astype(BF)
    prompt = added(keep, send(give, other_half())).astype(BF)
    doc, ret_2 = lax.optimization_barrier((doc, ret_2))
    mine = [send(doc, cross(0, 2)), send(doc, cross(1, 3))]
    docs = mine + [send(piece, other_core()) for piece in mine]
    prompts = [prompt] + [send(prompt, along_y(-k)) for k in (1, 2, 3)]
    gq, gk, gv = unpack([ret_0, ret_1, ret_2, ret_3])
    grad_doc, grad_prompt = finish(docs, prompts, w_key, w_value)
    return gq, gk, gv, grad_doc, grad_prompt


def solution(mesh):
    placed = (
        P("doc", None),
        P("prob", "resp", None),
        P(),
        P(),
        P(("doc", "resp", "prob"), None, None),
        P(("doc", "resp", "prob"), None, None),
        P(("doc", "resp", "prob"), None, None),
        P(("doc", "resp", "prob"), None, None),
        P(("doc", "resp", "prob")),
    )
    return jax.shard_map(
        on_device,
        mesh=mesh,
        in_specs=placed,
        out_specs=(
            P(("doc", "resp", "prob"), None, None),
            P(("doc", "resp", "prob"), None, None),
            P(("doc", "resp", "prob"), None, None),
            P("doc", None),
            P("prob", "resp", None),
        ),
        check_vma=False,
    )
```

```python
import jax
import jax.numpy as jnp
import numpy as np
from jax import lax
from jax.experimental import pallas as pl
from jax.experimental.pallas import tpu as pltpu
from jax.sharding import PartitionSpec as P

D = 5120
QH = 32
KVH = 4
HD = 128
R = 128
GROUP = QH // KVH
WIDE = GROUP * HD
KVW = 2 * HD
NZ = 4
DOC = 512
PROMPT = 1024
PRE = DOC + PROMPT
KEYS = PRE + R
SCALE = 1.0 / HD**0.5
LOG2E = 1.4426950408889634
MSG = 2 * WIDE + KVW + HD
RET = WIDE + KVW
BF = jnp.bfloat16
F32 = jnp.float32
TILE = 1024
VMEM = pl.BlockSpec(memory_space=pltpu.VMEM)
SMEM = pl.BlockSpec(memory_space=pltpu.SMEM)
ANY = pl.BlockSpec(memory_space=pl.ANY)


def live_block(length):
    rows = lax.broadcasted_iota(jnp.int32, (R, HD), 0)
    return jnp.where(rows < length, 1.0, 0.0).astype(BF)


def project_kernel(
    length, xd, xp, wk, wv, q, cot, rk, rv, msg_p, msg_m, msg_2, doc_0, doc_1, doc_2, own,
    xs, ws, qs, gs, ks, vs, acc, sems,
):
    y = lax.axis_index("doc")
    first = [
        pltpu.make_async_copy(xd, xs.at[pl.ds(0, R)], sems.at[0]),
        pltpu.make_async_copy(xp.at[0], xs.at[pl.ds(R, R)], sems.at[1]),
    ]
    parts = []
    for i in range(D // TILE):
        rows = pl.ds(i * TILE, TILE)
        parts.append(
            [
                pltpu.make_async_copy(wk.at[rows], ws.at[0, rows], sems.at[6 + 2 * i]),
                pltpu.make_async_copy(wv.at[rows], ws.at[1, rows], sems.at[7 + 2 * i]),
            ]
        )
    rest = [
        pltpu.make_async_copy(a.at[0], b, sems.at[2 + i])
        for i, (a, b) in enumerate(((q, qs), (cot, gs), (rk, ks), (rv, vs)))
    ]
    for c in first + sum(parts, []) + rest:
        c.start()
    for c in first:
        c.wait()
    for i, part_copies in enumerate(parts):
        for c in part_copies:
            c.wait()
        rows = slice(i * TILE, (i + 1) * TILE)
        x = xs[:, rows]
        for k in range(2):
            cols = slice(k * KVH * HD, (k + 1) * KVH * HD)
            term = jnp.dot(x, ws[k, rows, :], preferred_element_type=F32)
            acc[:, cols] = term if i == 0 else acc[:, cols] + term

    def head_pair(row, head):
        at = pl.multiple_of(head * HD, 128)
        return jnp.concatenate(
            [acc[row : row + R, pl.ds(at, HD)], acc[row : row + R, pl.ds(KVH * HD + at, HD)]], axis=1
        ).astype(BF)

    own[...] = head_pair(R, y)
    core = lax.rem(lax.axis_index("prob"), 2)
    for step, doc in ((0, doc_0), (1 + 2 * core, doc_1), (2, doc_2)):
        doc[...] = head_pair(0, lax.rem(y + step, 4))
    for c in rest:
        c.wait()
    live = live_block(length[0])
    for step, msg in ((1, msg_p), (3, msg_m), (2, msg_2)):
        head = lax.rem(y + step, 4)
        wide = pl.ds(pl.multiple_of(head * WIDE, 128), WIDE)
        thin = pl.ds(pl.multiple_of(head * HD, 128), HD)
        msg[:, :WIDE] = qs[:, wide]
        msg[:, WIDE : 2 * WIDE] = gs[:, wide]
        msg[:, 2 * WIDE : 2 * WIDE + HD] = ks[:, thin]
        msg[:, 2 * WIDE + HD : 2 * WIDE + KVW] = vs[:, thin]
        msg[:, MSG - HD : MSG] = live


def project(length, x_doc, x_prompt, w_key, w_value, q, cot, rk, rv):
    out = jax.ShapeDtypeStruct
    return pl.pallas_call(
        project_kernel,
        out_shape=(
            out((R, MSG), BF),
            out((R, MSG), BF),
            out((R, MSG), BF),
            out((R, KVW), BF),
            out((R, KVW), BF),
            out((R, KVW), BF),
            out((R, KVW), BF),
        ),
        in_specs=[SMEM] + [ANY] * 8,
        out_specs=[VMEM] * 7,
        scratch_shapes=[
            pltpu.VMEM((2 * R, D), BF),
            pltpu.VMEM((2, D, KVH * HD), BF),
            pltpu.VMEM((R, QH * HD), BF),
            pltpu.VMEM((R, QH * HD), BF),
            pltpu.VMEM((R, KVH * HD), BF),
            pltpu.VMEM((R, KVH * HD), BF),
            pltpu.VMEM((2 * R, 2 * KVH * HD), F32),
            pltpu.SemaphoreType.DMA((6 + 2 * (D // TILE),)),
        ],
        compiler_params=pltpu.CompilerParams(vmem_limit_bytes=56 * 2**20),
        cost_estimate=pl.CostEstimate(flops=2 * 256 * D * 1024, bytes_accessed=18 * 2**20, transcendentals=0),
        name="project",
    )(length, x_doc, x_prompt, w_key, w_value, q, cot, rk, rv)


CHUNK = 256
FIRST_COST = 5 * 10**9
MID_COST = 10**10
LAST_COST = 5 * 10**9


def attend_some(responses, kv, key_t, before, acc, own_acc, scores, dprobs):
    key_row = lax.broadcasted_iota(jnp.int32, (R, R), 0)
    query_col = lax.broadcasted_iota(jnp.int32, (R, R), 1)
    chunks = [(i, CHUNK) for i in range(0, PRE, CHUNK)] + [(PRE, R)]
    pairs = GROUP // 2
    items = [(r, j) for r in range(len(responses)) for j in range(pairs)]
    state = {}

    def prepare(i):
        r, j = items[i]
        q_of, g_of, own, live, ret = responses[r]
        if j == 0:
            allowed = (key_row <= query_col) & live
            state["own", r] = own, own[:, :HD].T, jnp.concatenate([allowed, allowed], axis=1)
        two_q, two_g = q_of(j), g_of(j)
        nought = jnp.zeros((R, HD), BF)
        q0, q1 = two_q[:, :HD], two_q[:, HD:]
        g0 = jnp.where(live, two_g[:, :HD], nought)
        g1 = jnp.where(live, two_g[:, HD:], nought)
        state[i] = dict(
            q_rows=jnp.concatenate([q0, q1], axis=0),
            g_rows=jnp.concatenate([g0, g1], axis=0),
            q_t=jnp.concatenate([q0.T, q1.T], axis=1),
            g_t=jnp.concatenate([g0.T, g1.T], axis=1),
            peak=None,
            total=jnp.zeros((1, KVW), F32),
            delta=jnp.zeros((1, KVW), F32),
            dq_t=jnp.zeros((HD, KVW), F32),
        )

    def step_a(i, start, size):
        st = state[i]
        own, _, allowed = state["own", items[i][0]]
        keys = own[:, :HD] if start == PRE else kv[start : start + size, :HD]
        s = jnp.dot(keys, st["q_t"], preferred_element_type=F32)
        if start == PRE:
            s = jnp.where(allowed, s, -1e30)
        scores[i % 2, start : start + size, :] = s
        top = jnp.max(s, axis=0, keepdims=True)
        st["peak"] = top if st["peak"] is None else jnp.maximum(st["peak"], top)

    def end_a(i):
        state[i]["shift"] = state[i]["peak"] * (SCALE * LOG2E)

    def step_b(i, start, size):
        st = state[i]
        rows = slice(start, start + size)
        values = state["own", items[i][0]][0][:, HD:] if start == PRE else kv[rows, HD:]
        e = jnp.exp2(scores[i % 2, rows, :] * (SCALE * LOG2E) - st["shift"])
        dp = jnp.dot(values, st["g_t"], preferred_element_type=F32)
        st["total"] += jnp.sum(e, axis=0, keepdims=True)
        st["delta"] += jnp.sum(e * dp, axis=0, keepdims=True)
        scores[i % 2, rows, :] = e
        dprobs[i % 2, rows, :] = dp

    def end_b(i):
        state[i]["inv"] = 1.0 / state[i]["total"]
        state[i]["delta"] = state[i]["delta"] * state[i]["inv"]

    def step_c(i, start, size):
        st = state[i]
        r, j = items[i]
        rows = slice(start, start + size)
        p = scores[i % 2, rows, :] * st["inv"]
        ds = (p * (dprobs[i % 2, rows, :] - st["delta"])).astype(BF)
        dk = jnp.dot(ds, st["q_rows"], preferred_element_type=F32)
        dv = jnp.dot(p.astype(BF), st["g_rows"], preferred_element_type=F32)
        if start == PRE:
            where, old = own_acc, own_acc if j else None
            rows = slice(0, R)
            left = state["own", r][1]
        else:
            where, old = acc, acc if i else before
            left = key_t[:, rows]
        where[rows, :HD] = dk if old is None else old[rows, :HD] + dk
        where[rows, HD:] = dv if old is None else old[rows, HD:] + dv
        st["dq_t"] += jnp.dot(left, ds, preferred_element_type=F32)

    def end_c(i):
        r, j = items[i]
        ret = responses[r][4]
        dq_t = state[i]["dq_t"] * SCALE
        ret[:, j * KVW : (j + 1) * KVW] = jnp.concatenate([dq_t[:, :HD].T, dq_t[:, HD:].T], axis=1).astype(BF)
        if j == pairs - 1:
            ret[:, WIDE:] = scaled(own_acc[...])

    n = len(items)
    for i in range(-1, n):
        if i + 1 < n:
            prepare(i + 1)
        for c in chunks:
            if i >= 0:
                step_b(i, *c)
            if i + 1 < n:
                step_a(i + 1, *c)
        if i + 1 < n:
            end_a(i + 1)
        if i >= 0:
            end_b(i)
            for c in chunks:
                step_c(i, *c)
            end_c(i)


def scaled(block):
    col = lax.broadcasted_iota(jnp.int32, block.shape, 1)
    return (block * jnp.where(col < HD, SCALE, 1.0)).astype(BF)


def bundled(msg, ret):
    def q_of(j):
        return msg[:, j * KVW : (j + 1) * KVW]

    def g_of(j):
        return msg[:, WIDE + j * KVW : WIDE + (j + 1) * KVW]

    return q_of, g_of, msg[:, 2 * WIDE : 2 * WIDE + KVW], msg[:, MSG - HD :] > 0, ret


def attend_first_kernel(
    length, q, cot, rk, rv, doc_0, mine, other, doc_2, z0, z1, z2, z3,
    ret, kv, key_t, acc, own_acc, scores, dprobs,
):
    core = lax.rem(lax.axis_index("prob"), 2)
    for row, piece in ((0, doc_0), (3 - 2 * core, mine), (1 + 2 * core, other), (2, doc_2)):
        kv[pl.ds(pl.multiple_of(row * R, R), R), :] = piece[...]
    for k, block in enumerate((z0, z1, z2, z3)):
        kv[DOC + 2 * R * k : DOC + 2 * R * (k + 1), :] = block[...]
    key_t[...] = kv[:, :HD].T
    head = lax.axis_index("doc")

    def q_of(j):
        return q[0, :, pl.ds(pl.multiple_of(head * WIDE + j * KVW, 128), KVW)]

    def g_of(j):
        return cot[0, :, pl.ds(pl.multiple_of(head * WIDE + j * KVW, 128), KVW)]

    thin = pl.ds(pl.multiple_of(head * HD, 128), HD)
    own = jnp.concatenate([rk[0, :, thin], rv[0, :, thin]], axis=1)
    live = live_block(length[0]) > 0
    attend_some([(q_of, g_of, own, live, ret)], kv, key_t, None, acc, own_acc, scores, dprobs)


def attend_mid_kernel(msg_m, msg_p, kv, key_t, before, ret_m, ret_p, acc, ret, own_acc, scores, dprobs):
    acc[...] = before[...]

    def response(r, carry):
        def either(start, size):
            cols = slice(start, start + size)
            return jnp.where(r == 0, msg_m[:, cols], msg_p[:, cols])

        def q_of(j):
            return either(j * KVW, KVW)

        def g_of(j):
            return either(WIDE + j * KVW, KVW)

        live = either(MSG - HD, HD) > 0
        one = q_of, g_of, either(2 * WIDE, KVW), live, ret
        attend_some([one], kv, key_t, acc, acc, own_acc, scores, dprobs)

        @pl.when(r == 0)
        def _():
            ret_m[...] = ret[...]

        @pl.when(r == 1)
        def _():
            ret_p[...] = ret[...]

        return carry

    lax.fori_loop(0, 2, response, 0)


def attend_last_kernel(msg_2, kv, key_t, before, ret_2, m0, m1, m2, m3, acc, own_acc, scores, dprobs):
    attend_some([bundled(msg_2, ret_2)], kv, key_t, before, acc, own_acc, scores, dprobs)
    y, z = lax.axis_index("doc"), lax.axis_index("resp") // 2
    for k, out in enumerate((m0, m1, m2, m3)):
        rows = pl.ds(pl.multiple_of(lax.rem(z + k - y + 4, 4) * R, R), R)
        out[:R] = scaled(acc[rows, :])
        out[R:] = scaled(acc[DOC + 2 * R * k : DOC + 2 * R * (k + 1), :])


RET_SHAPE = jax.ShapeDtypeStruct((R, RET), BF)
ACC_SHAPE = jax.ShapeDtypeStruct((PRE, KVW), F32)


def attend(kernel, name, count, in_specs, outs, scratch, *args):
    return pl.pallas_call(
        kernel,
        out_shape=outs,
        in_specs=in_specs,
        out_specs=[VMEM] * len(outs),
        scratch_shapes=scratch
        + [pltpu.VMEM((R, KVW), F32), pltpu.VMEM((2, KEYS, KVW), F32), pltpu.VMEM((2, KEYS, KVW), F32)],
        compiler_params=pltpu.CompilerParams(vmem_limit_bytes=24 * 2**20),
        cost_estimate=pl.CostEstimate(
            flops=count, bytes_accessed=0, transcendentals=0
        ),
        name=name,
    )(*args)


def attend_first(length, q, cot, rk, rv, docs, zs):
    out = jax.ShapeDtypeStruct
    outs = [RET_SHAPE, out((PRE, KVW), BF), out((HD, PRE), BF), ACC_SHAPE]
    specs = [SMEM] + [VMEM] * 12
    return attend(attend_first_kernel, "attend_first", FIRST_COST, specs, outs, [], length, q, cot, rk, rv, *docs, *zs)


def attend_mid(msg_m, msg_p, kv, key_t, acc):
    outs = [RET_SHAPE, RET_SHAPE, ACC_SHAPE]
    scratch = [pltpu.VMEM((R, RET), BF)]
    return attend(attend_mid_kernel, "attend_mid", MID_COST, [VMEM] * 5, outs, scratch, msg_m, msg_p, kv, key_t, acc)


def attend_last(msg_2, kv, key_t, acc):
    outs = [RET_SHAPE] + [jax.ShapeDtypeStruct((3 * R, KVW), BF)] * 4
    scratch = [pltpu.VMEM((PRE, KVW), F32)]
    return attend(attend_last_kernel, "attend_last", LAST_COST, [VMEM] * 4, outs, scratch, msg_2, kv, key_t, acc)


def unpack_kernel(r0, r1, r2, r3, gq, gk, gv):
    for k, r in enumerate((r0, r1, r2, r3)):
        head = lax.rem(lax.axis_index("doc") + k, 4)
        thin = pl.ds(pl.multiple_of(head * HD, 128), HD)
        gq[0, :, pl.ds(pl.multiple_of(head * WIDE, 128), WIDE)] = r[:, :WIDE]
        gk[0, :, thin] = r[:, WIDE : WIDE + HD]
        gv[0, :, thin] = r[:, WIDE + HD :]


def unpack(rets):
    out = jax.ShapeDtypeStruct
    return pl.pallas_call(
        unpack_kernel,
        out_shape=(out((1, R, QH * HD), BF), out((1, R, KVH * HD), BF), out((1, R, KVH * HD), BF)),
        in_specs=[VMEM] * 4,
        out_specs=[VMEM] * 3,
        compiler_params=pltpu.CompilerParams(vmem_limit_bytes=12 * 2**20),
        cost_estimate=pl.CostEstimate(flops=0, bytes_accessed=2**22, transcendentals=0),
        name="unpack",
    )(*rets)


def finish_kernel(d0, d1, d2, d3, p0, p1, p2, p3, wk, wv, grad_doc, grad_prompt, left, out, sems):
    y, z, core = lax.axis_index("doc"), lax.axis_index("resp") // 2, lax.axis_index("prob") % 2
    for k, (doc, prompt) in enumerate(((d0, p0), (d1, p1), (d2, p2), (d3, p3))):
        step = lax.rem(2 * core + k, 4)
        for row, piece, head in ((0, doc, lax.rem(z + 4 - step, 4)), (R, prompt, lax.rem(y + k, 4))):
            at = pl.multiple_of(head * HD, 128)
            left[row : row + R, pl.ds(at, HD)] = piece[:, :HD]
            left[row : row + R, pl.ds(KVH * HD + at, HD)] = piece[:, HD:]
    over = (((1,), (1,)), ((), ()))
    copies = []
    for i in range(D // TILE):
        cols = slice(i * TILE, (i + 1) * TILE)
        total = lax.dot_general(left[:, : KVH * HD], wk[cols, :], over, preferred_element_type=F32)
        total += lax.dot_general(left[:, KVH * HD :], wv[cols, :], over, preferred_element_type=F32)
        out[:, cols] = total.astype(BF)
        cols = pl.ds(i * TILE, TILE)
        copies += [
            pltpu.make_async_copy(out.at[pl.ds(0, R), cols], grad_doc.at[:, cols], sems.at[2 * i]),
            pltpu.make_async_copy(out.at[pl.ds(R, R), cols], grad_prompt.at[0, :, cols], sems.at[2 * i + 1]),
        ]
        copies[-2].start()
        copies[-1].start()
    for c in copies:
        c.wait()


def finish(docs, prompts, w_key, w_value):
    out = jax.ShapeDtypeStruct
    return pl.pallas_call(
        finish_kernel,
        out_shape=(out((R, D), BF), out((1, R, D), BF)),
        in_specs=[VMEM] * 10,
        out_specs=[ANY, ANY],
        scratch_shapes=[
            pltpu.VMEM((2 * R, 2 * KVH * HD), BF),
            pltpu.VMEM((2 * R, D), BF),
            pltpu.SemaphoreType.DMA((2 * (D // TILE),)),
        ],
        compiler_params=pltpu.CompilerParams(vmem_limit_bytes=20 * 2**20),
        cost_estimate=pl.CostEstimate(flops=2 * 256 * D * 1024, bytes_accessed=18 * 2**20, transcendentals=0),
        name="finish",
    )(*docs, *prompts, w_key, w_value)


def moves(axes, rule):
    sizes = [lax.axis_size(a) for a in axes]
    pairs = []
    for index in range(np.prod(sizes)):
        here = np.unravel_index(index, sizes)
        there = rule(*(int(i) for i in here))
        pairs.append((index, int(np.ravel_multi_index(there, sizes))))
    return (axes if len(axes) > 1 else axes[0]), pairs


def send(x, move):
    return lax.ppermute(x, *move)


def along_y(k):
    return moves(("doc",), lambda y: ((y + k) % 4,))


def turned(resp, k):
    return ((resp // 2 + k) % NZ) * 2 + resp % 2


def beside_y():
    return moves(("doc", "prob"), lambda y, p: ((y + 1 + 2 * (p % 2)) % 4, p))


def along_z(k):
    return moves(("resp",), lambda r: (turned(r, k),))


def along_x(k):
    def rule(resp, prob):
        x = ((resp % 2) * 2 + prob // 2 + k) % 4
        return (resp // 2) * 2 + x // 2, (x % 2) * 2 + prob % 2

    return moves(("resp", "prob"), rule)


def other_half():
    return moves(("resp",), lambda r: (r ^ 1,))


def other_core():
    return moves(("prob",), lambda p: (p ^ 1,))


def cross(first, second):
    def rule(y, resp, prob):
        k = first if prob % 2 == 0 else second
        return resp // 2, ((y + k) % 4) * 2 + resp % 2, prob

    return moves(("doc", "resp", "prob"), rule)


def added(*pieces):
    total = pieces[0].astype(F32)
    for piece in pieces[1:]:
        total = total + piece.astype(F32)
    return total


def sum_kernel(m0, m1, m2, m3, doc, keep, give):
    total = added(m0[...], m1[...], m2[...], m3[...])
    doc[...] = total[:R].astype(BF)
    keep[...] = total[R : 2 * R]
    give[...] = total[2 * R :].astype(BF)


def sum_blocks(blocks):
    out = jax.ShapeDtypeStruct
    return pl.pallas_call(
        sum_kernel,
        out_shape=(out((R, KVW), BF), out((R, KVW), F32), out((R, KVW), BF)),
        in_specs=[VMEM] * 4,
        out_specs=[VMEM] * 3,
        compiler_params=pltpu.CompilerParams(vmem_limit_bytes=8 * 2**20),
        cost_estimate=pl.CostEstimate(flops=2**18, bytes_accessed=2**20, transcendentals=0),
        name="sum_blocks",
    )(*blocks)


def on_device(x_doc, x_prompt, w_key, w_value, queries, resp_keys, resp_values, out_grad, lengths):
    msg_p, msg_m, msg_2, doc_0, doc_1, doc_2, own = project(
        lengths, x_doc, x_prompt, w_key, w_value, queries, out_grad, resp_keys, resp_values
    )
    half = send(own, other_half())
    doc_1 = send(doc_1, beside_y())
    doc_2 = send(doc_2, along_y(2))
    half, doc_2 = lax.optimization_barrier((half, doc_2))
    docs = [doc_0, doc_1, send(doc_1, other_core()), doc_2]
    block = jnp.concatenate([own, half], axis=0)
    blocks = [block] + [send(block, along_z(-k)) for k in (1, 2, 3)]
    msg_p = send(msg_p, along_y(1))
    msg_m = send(msg_m, along_y(-1))
    msg_2 = send(msg_2, along_y(2))
    ret_0, kv, key_t, acc = attend_first(
        lengths, queries, out_grad, resp_keys, resp_values, docs, blocks
    )
    ret_m, ret_p, acc = attend_mid(msg_m, msg_p, kv, key_t, acc)
    ret_1 = send(ret_p, along_y(-1))
    ret_3 = send(ret_m, along_y(1))
    ret_2, *terms = attend_last(msg_2, kv, key_t, acc)
    ret_2 = send(ret_2, along_y(2))
    blocks = [terms[0]] + [send(terms[k], along_z(k)) for k in (1, 2, 3)]
    blocks, ret_1, ret_3 = lax.optimization_barrier((blocks, ret_1, ret_3))
    doc, keep, give = sum_blocks(blocks)
    doc = added(doc, send(doc, other_core())).astype(BF)
    doc = added(doc, *(send(doc, along_x(k)) for k in (1, 2, 3))).astype(BF)
    prompt = added(keep, send(give, other_half())).astype(BF)
    prompt, ret_2 = lax.optimization_barrier((prompt, ret_2))
    mine = [send(doc, cross(0, 2)), send(doc, cross(1, 3))]
    docs = mine + [send(piece, other_core()) for piece in mine]
    prompts = [prompt] + [send(prompt, along_y(-k)) for k in (1, 2, 3)]
    gq, gk, gv = unpack([ret_0, ret_1, ret_2, ret_3])
    grad_doc, grad_prompt = finish(docs, prompts, w_key, w_value)
    return gq, gk, gv, grad_doc, grad_prompt


def solution(mesh):
    placed = (
        P("doc", None),
        P("prob", "resp", None),
        P(),
        P(),
        P(("doc", "resp", "prob"), None, None),
        P(("doc", "resp", "prob"), None, None),
        P(("doc", "resp", "prob"), None, None),
        P(("doc", "resp", "prob"), None, None),
        P(("doc", "resp", "prob")),
    )
    return jax.shard_map(
        on_device,
        mesh=mesh,
        in_specs=placed,
        out_specs=(
            P(("doc", "resp", "prob"), None, None),
            P(("doc", "resp", "prob"), None, None),
            P(("doc", "resp", "prob"), None, None),
            P("doc", None),
            P("prob", "resp", None),
        ),
        check_vma=False,
    )
```
